32 devices in a mesh: chan: 16 (over z, x, core), win: 2 (over y).
Axes of the slice: x: 2, y: 2, z: 4, core: 2. Of those that a mesh axis runs over, the one named last changes fastest.
Arguments:
- strain_rate: bfloat16 [2, 1024, 8192], P('win', 'chan'), may hold values from -600 to 600
- bandpass_taps: bfloat16 [65], replicated, may hold values from -0.75 to 0.75
- pair_offsets: int32 [16, 6], P('chan'), may hold values from -1 to 15, as said below
- lag_limit: int32 [16, 6], P('chan'), may hold values from 1 to 8
Outputs:
- correlations: float32 [6, 8192, 2176], P(None, ('chan', 'win'))
The draws below stay inside these ranges and needn't reach their ends.
Inputs may be any that keep to these rules, and one draw needn't show every extreme that they name: `pair_offsets`: row b lists distinct block offsets o (partner block (b + o) mod 16) in its first slots and -1 in the remaining slots; every row has at least one offset, some row uses all 6 slots and some row only one.
All inputs are finite; a program needn't handle non-finite values.
Results may differ from the reference program's by a relative error of at most 0.0027.
Values may be sent and summed in bfloat16 or wider, within the bound.
A program may use at most 128 MiB of HBM per device.

```python
import math
import jax
import jax.numpy as jnp
from jax import lax

CHANNELS = 8192
NBLOCKS = 16
VIRTUAL_SOURCES = 128
SEGMENT_LENGTH = 1024
HALF = 32
MAXIMUM_LAG = 8
SLOTS = 6
N_CHAN = 16
N_WIN = 2


def draw_strain_rate(key, part):
    sensor_scaling_seed, transient_seed, ambient_random_seed = jax.random.split(key, 3)
    channel_gain = jnp.exp(jax.random.uniform(sensor_scaling_seed, (CHANNELS,), jnp.float32, 0.0, math.log(10.0)))
    transient_spikes = jnp.exp(jax.random.uniform(transient_seed, (N_WIN, SEGMENT_LENGTH // 32), jnp.float32, 0.0, math.log(10.0)))
    smooth_magnitude_curve = jnp.repeat(transient_spikes, 32, axis=1)
    noise_field = jax.random.truncated_normal(ambient_random_seed, -6.0, 6.0, (N_WIN, SEGMENT_LENGTH, CHANNELS), jnp.float32)
    return (noise_field * smooth_magnitude_curve[:, :, None] * channel_gain[None, None, :]).astype(jnp.bfloat16)


def draw_pair_offsets(key, part):
    key_score, key_full, key_single, key_busy, key_few = jax.random.split(key, 5)
    row_ids = jnp.arange(NBLOCKS, dtype=jnp.int32)
    scores = jax.random.randint(key_score, (NBLOCKS, NBLOCKS), 0, 2 ** 20, jnp.int32) * NBLOCKS + row_ids[None, :]
    full_row = jax.random.randint(key_full, (), 0, NBLOCKS, jnp.int32)
    single = (full_row + 1 + jax.random.randint(key_single, (), 0, NBLOCKS - 1, jnp.int32)) % NBLOCKS
    last_column = row_ids == NBLOCKS - 1
    scores = jnp.where((row_ids[:, None] == full_row) & last_column[None, :], -1, scores)
    ranked = jnp.argsort(scores, axis=1, stable=True)[:, :SLOTS].astype(jnp.int32)
    busy_rows = jax.random.randint(key_busy, (NBLOCKS,), 0, 4, jnp.int32) == 0
    few_slots = jax.random.randint(key_few, (NBLOCKS,), 1, 3, jnp.int32)
    used_slots = jnp.where(busy_rows, SLOTS, few_slots)
    used_slots = jnp.where(row_ids == full_row, SLOTS, used_slots)
    used_slots = jnp.where(row_ids == single, 1, used_slots)
    slot_ids = jnp.arange(SLOTS, dtype=jnp.int32)
    return jnp.where(slot_ids[None, :] < used_slots[:, None], ranked, -1).astype(jnp.int32)


def set_ends(array, own_key, low, top_value):
    extent = array.shape
    spot = [jax.random.randint(jax.random.fold_in(own_key, axis), (), 0, extent[axis]) for axis in range(len(extent))]
    array = array.at[tuple(spot)].set(low)
    longest = extent.index(max(extent))
    spot[longest] = (spot[longest] + 1) % extent[longest]
    return array.at[tuple(spot)].set(top_value)


def centred(key, extent, width, limit, held_as=jnp.bfloat16):
    values = width * jax.random.normal(key, extent, jnp.float32)
    return jnp.clip(values, min=-limit, max=limit).astype(held_as)


def setup_inputs(seed: int = 0) -> dict:
    keys = jax.random.split(jax.random.key(seed), 5)
    return {
        "strain_rate": draw_strain_rate(jax.random.fold_in(keys[4], 71), 0),
        "bandpass_taps": centred(keys[1], (2 * HALF + 1,), (2 * HALF + 1) ** -0.5, 0.75),
        "pair_offsets": draw_pair_offsets(jax.random.fold_in(keys[4], 71), 0),
        "lag_limit": set_ends(jax.random.randint(keys[3], (NBLOCKS, SLOTS), 1, MAXIMUM_LAG + 1), jax.random.fold_in(keys[3], 1), 1, MAXIMUM_LAG).astype(jnp.int32),
    }


def band_filter(values, taps):
    samples, channel_count = values.shape
    tap_count = taps.shape[0]
    half_width = (tap_count - 1) // 2
    block_len = min(256, samples)
    pieces = samples // block_len
    padded = jnp.pad(values, ((half_width, half_width), (0, 0)))
    head_rows = padded[:samples].reshape(pieces, block_len, channel_count)
    rest_rows = jnp.pad(padded[block_len:], ((0, block_len - 2 * half_width), (0, 0)))
    tail_rows = rest_rows.reshape(pieces, block_len, channel_count)[:, :2 * half_width]
    window = jnp.concatenate([head_rows, tail_rows], axis=1)
    period = jnp.concatenate([taps, jnp.zeros((block_len,), taps.dtype)])
    matrix = jnp.tile(period, block_len)[:block_len * (block_len + 2 * half_width)]
    matrix = matrix.reshape(block_len, block_len + 2 * half_width)
    filtered = jnp.einsum('ij,bjc->bic', matrix.astype(jnp.float32), window.astype(jnp.float32), precision=lax.Precision.HIGHEST)
    return filtered.reshape(samples, channel_count)

def normalize(window, taps):
    filtered = band_filter(window, taps)
    tap_count = taps.shape[0]
    magnitude = lax.optimization_barrier(jnp.abs(filtered).astype(jnp.bfloat16))
    box_taps = jnp.ones((tap_count,), jnp.bfloat16)
    mean_level = band_filter(magnitude, box_taps) * (1.0 / tap_count)
    return (filtered / (mean_level + 1e-05)).astype(jnp.bfloat16)

def lagged(source_traces, samples):
    padded = jnp.pad(source_traces, ((0, 0), (0, 0), (MAXIMUM_LAG, MAXIMUM_LAG)))
    lag_rows = [padded[:, :, lag_index:lag_index + samples] for lag_index in range(2 * MAXIMUM_LAG + 1)]
    return jnp.concatenate(lag_rows, axis=1)

def reference(strain_rate, bandpass_taps, pair_offsets, lag_limit):
    blocks = N_CHAN
    channel_count = CHANNELS // blocks
    source_spacing = channel_count // VIRTUAL_SOURCES
    column_list = (2 * MAXIMUM_LAG + 1) * VIRTUAL_SOURCES
    cleaned = lax.map(lambda window: normalize(window, bandpass_taps), strain_rate)
    source_channels = jnp.swapaxes(cleaned[:, :, ::source_spacing], 1, 2)
    lag_samples = jnp.arange(column_list, dtype=jnp.int32) // VIRTUAL_SOURCES - MAXIMUM_LAG

    def per_block(block_id):
        receivers = lax.dynamic_slice_in_dim(cleaned, block_id * channel_count, channel_count, 2).astype(jnp.float32)
        results = []
        for slot_index in range(SLOTS):
            offset_now = pair_offsets[block_id, slot_index]
            limit_now = lag_limit[block_id, slot_index]

            def compute(unused):
                paired_block = ((block_id + offset_now) % blocks).astype(jnp.int32)
                source_traces = lax.dynamic_slice_in_dim(source_channels, (paired_block * VIRTUAL_SOURCES).astype(jnp.int32), VIRTUAL_SOURCES, 1)
                stacked = lagged(source_traces, SEGMENT_LENGTH).astype(receivers.dtype)
                product = jnp.einsum('wtr,wct->rc', receivers, stacked, precision=lax.Precision.HIGHEST)
                lag_mask = (jnp.abs(lag_samples) <= limit_now).astype(receivers.dtype)
                return product * lag_mask[None, :]

            def nothing(unused):
                return jnp.zeros((channel_count, column_list), receivers.dtype)
            results.append(lax.cond(offset_now >= 0, compute, nothing, 0))
        return jnp.stack(results)
    result = lax.map(per_block, jnp.arange(blocks, dtype=jnp.int32))
    factor = 1.0 / math.sqrt(SEGMENT_LENGTH * N_WIN)
    return jnp.transpose(result, (1, 0, 2, 3)).reshape(SLOTS, CHANNELS, column_list) * factor
```

```python
import functools
import math

import jax
import jax.numpy as jnp
from jax import lax
from jax.experimental import pallas as pl
from jax.experimental.pallas import tpu as pltpu
from jax.sharding import PartitionSpec as P

VIRTUAL_SOURCES = 128
MAXIMUM_LAG = 8
LAGS = 2 * MAXIMUM_LAG + 1
PIECE = 256
REACH = 384
VMEM_LIMIT = 48 * 1024 * 1024


def band(row, half):
    wide = jnp.broadcast_to(row, (PIECE, REACH))
    return pltpu.roll(wide, 0, 1, stride=1, stride_axis=0).astype(jnp.bfloat16)


def normalize_kernel(half, taps_ref, x_ref, out_ref, src_ref, padded, level, filtered):
    parts, _, rows, channels = x_ref.shape
    samples = parts * rows
    tap_count = 2 * half + 1
    tail = padded.shape[0] - samples - half
    padded[:half] = jnp.zeros((half, channels), jnp.bfloat16)
    padded[half + samples :] = jnp.zeros((tail, channels), jnp.bfloat16)
    level[:half] = jnp.zeros((half, channels), jnp.bfloat16)
    level[half + samples :] = jnp.zeros((tail, channels), jnp.bfloat16)
    for i in range(parts):
        padded[half + i * rows : half + (i + 1) * rows] = x_ref[i, 0]
    taps = band(taps_ref[...], half)
    ones = jnp.where(
        lax.broadcasted_iota(jnp.int32, (1, REACH), 1) < tap_count, 1.0, 0.0
    ).astype(jnp.float32)
    box = band(ones, half)
    for p in range(samples // PIECE):
        low = p * PIECE
        value = jnp.dot(taps, padded[low : low + REACH], preferred_element_type=jnp.float32)
        filtered[low : low + PIECE] = value
        level[half + low : half + low + PIECE] = jnp.abs(value).astype(jnp.bfloat16)
    per = src_ref.shape[0]
    spacing = channels // per
    pick = (
        lax.broadcasted_iota(jnp.int32, (per, channels), 1)
        == spacing * lax.broadcasted_iota(jnp.int32, (per, channels), 0)
    )
    pick = jnp.where(pick, 1.0, 0.0).astype(jnp.bfloat16)
    for p in range(samples // PIECE):
        low = p * PIECE
        total = jnp.dot(box, level[low : low + REACH], preferred_element_type=jnp.float32)
        mean = total * (1.0 / tap_count)
        value = filtered[low : low + PIECE] / (mean + 1e-05)
        turned = jnp.transpose(value).astype(jnp.bfloat16)
        out_ref[:, low : low + PIECE] = turned
        src_ref[:, low : low + PIECE] = jnp.dot(
            pick, turned, preferred_element_type=jnp.float32
        ).astype(jnp.bfloat16)


def normalize(parts, taps):
    blocks, windows, rows, channels = parts.shape
    samples = blocks * rows
    half = (taps.shape[0] - 1) // 2
    sources = VIRTUAL_SOURCES // windows
    row = jnp.pad(taps.astype(jnp.float32), (0, REACH - taps.shape[0]))[None]
    return pl.pallas_call(
        functools.partial(normalize_kernel, half),
        grid=(windows,),
        out_shape=(
            jax.ShapeDtypeStruct((channels, windows * samples), jnp.bfloat16),
            jax.ShapeDtypeStruct((sources, windows * samples), jnp.bfloat16),
        ),
        in_specs=[
            pl.BlockSpec((1, REACH), lambda w: (0, 0)),
            pl.BlockSpec((blocks, 1, rows, channels), lambda w: (0, w, 0, 0)),
        ],
        out_specs=(
            pl.BlockSpec((channels, samples), lambda w: (0, w)),
            pl.BlockSpec((sources, samples), lambda w: (0, w)),
        ),
        scratch_shapes=[
            pltpu.VMEM((samples + REACH - PIECE, channels), jnp.bfloat16),
            pltpu.VMEM((samples + REACH - PIECE, channels), jnp.bfloat16),
            pltpu.VMEM((samples, channels), jnp.float32),
        ],
        compiler_params=pltpu.CompilerParams(vmem_limit_bytes=VMEM_LIMIT),
        name="normalize",
    )(row, parts)


def shift_kernel(x_ref, out_ref):
    rows, samples = x_ref.shape
    value = x_ref[...].astype(jnp.float32)
    spot = lax.broadcasted_iota(jnp.int32, (rows, samples), 1)
    for index in range(LAGS):
        lag = index - MAXIMUM_LAG
        if lag == 0:
            moved = value
        else:
            moved = pltpu.roll(value, lag % samples, 1)
            kept = spot >= lag if lag > 0 else spot < samples + lag
            moved = jnp.where(kept, moved, 0.0)
        out_ref[index] = moved.astype(jnp.bfloat16)


def shift(receivers, windows):
    channels, length = receivers.shape
    samples = length // windows
    rows = min(32, channels)
    return pl.pallas_call(
        shift_kernel,
        grid=(channels // rows, windows),
        out_shape=jax.ShapeDtypeStruct((LAGS, channels, length), jnp.bfloat16),
        in_specs=[pl.BlockSpec((rows, samples), lambda c, w: (c, w))],
        out_specs=pl.BlockSpec((LAGS, rows, samples), lambda c, w: (0, c, w)),
        compiler_params=pltpu.CompilerParams(vmem_limit_bytes=VMEM_LIMIT),
        cost_estimate=pl.CostEstimate(
            flops=2 * LAGS * channels * length,
            bytes_accessed=2 * (LAGS + 1) * channels * length,
            transcendentals=0,
        ),
        name="shift",
    )(receivers)


def correlate_kernel(factor, partner, limit, lhs_ref, *refs):
    source_refs, out_ref = refs[:-1], refs[-1]
    slots = len(source_refs)
    lag = jnp.abs(pl.program_id(0) - MAXIMUM_LAG)
    for first in range(0, slots, 2):
        group = range(first, min(first + 2, slots))
        reach = functools.reduce(jnp.maximum, [limit[k] for k in group])

        @pl.when(lag <= reach)
        def _():
            panel = jnp.concatenate([source_refs[k][0] for k in group], axis=0)
            product = lax.dot_general(
                lhs_ref[0], panel, (((1,), (1,)), ((), ())), preferred_element_type=jnp.float32
            )
            for i, k in enumerate(group):
                piece = product[:, i * VIRTUAL_SOURCES : (i + 1) * VIRTUAL_SOURCES]
                out_ref[k] = jnp.where(lag <= limit[k], piece * factor, 0.0)

        @pl.when(lag > reach)
        def _():
            for k in group:
                out_ref[k] = jnp.zeros(out_ref.shape[1:], jnp.float32)


def correlate(lagged, gathered, partner, limit):
    _, channels, length = lagged.shape
    slots = partner.shape[0]

    def source_spec(k):
        return pl.BlockSpec(
            (1, VIRTUAL_SOURCES, length), lambda l, partner, limit: (partner[k], 0, 0)
        )

    return pl.pallas_call(
        functools.partial(correlate_kernel, 1.0 / math.sqrt(length)),
        grid_spec=pltpu.PrefetchScalarGridSpec(
            num_scalar_prefetch=2,
            grid=(LAGS,),
            in_specs=[pl.BlockSpec((1, channels, length), lambda l, partner, limit: (l, 0, 0))]
            + [source_spec(k) for k in range(slots)],
            out_specs=pl.BlockSpec(
                (slots, channels, VIRTUAL_SOURCES), lambda l, partner, limit: (0, 0, l)
            ),
        ),
        out_shape=jax.ShapeDtypeStruct((slots, channels, LAGS * VIRTUAL_SOURCES), jnp.float32),
        compiler_params=pltpu.CompilerParams(vmem_limit_bytes=VMEM_LIMIT),
        name="correlate",
    )(partner, limit, lagged, *[gathered] * slots)


def gather(sources, blocks):
    gathered = lax.all_gather(sources, ("chan", "win"))
    return gathered.reshape(blocks, VIRTUAL_SOURCES, sources.shape[1])


def gather_by_window(sources, partner, windows):
    samples = sources.shape[1] // windows
    blocks = lax.axis_size("chan")

    def one(window, panels):
        mine = lax.dynamic_slice_in_dim(sources, window * samples, samples, 1)
        mine = lax.all_gather(mine, "win", tiled=True)
        taken = lax.all_gather(mine, "chan")[partner]
        return lax.dynamic_update_slice_in_dim(panels, taken, window * samples, 2)

    empty = jnp.zeros((partner.shape[0], VIRTUAL_SOURCES, sources.shape[1]), sources.dtype)
    return lax.fori_loop(0, windows, one, empty)


def on_device(strain_rate, bandpass_taps, pair_offsets, lag_limit):
    blocks, windows = lax.axis_size("chan"), lax.axis_size("win")
    _, rows, total = strain_rate.shape
    channels = total // (blocks * windows)
    parts = lax.all_to_all(
        strain_rate[0], ("chan", "win"), split_axis=1, concat_axis=0, tiled=True
    ).reshape(blocks, windows, rows, channels)
    receivers, sources = normalize(parts, bandpass_taps)
    lagged = shift(receivers, windows)
    offsets = pair_offsets[0]
    used = offsets >= 0
    partner = jnp.where(used, (lax.axis_index("chan") + offsets) % blocks, 0).astype(jnp.int32)
    limit = jnp.where(used, lag_limit[0], -1).astype(jnp.int32)
    if windows > 2:
        panels = gather_by_window(sources, partner, windows)
        return correlate(lagged, panels, jnp.arange(partner.shape[0], dtype=jnp.int32), limit)
    return correlate(lagged, gather(sources, blocks), partner, limit)


def solution(mesh):
    placed = (P("win", "chan", None), P(), P("chan", None), P("chan", None))
    return jax.shard_map(
        on_device,
        mesh=mesh,
        in_specs=placed,
        out_specs=P(None, ("chan", "win"), None),
        check_vma=False,
    )
```

```python
import functools
import math

import jax
import jax.numpy as jnp
from jax import lax
from jax.experimental import pallas as pl
from jax.experimental.pallas import tpu as pltpu
from jax.sharding import PartitionSpec as P

VIRTUAL_SOURCES = 128
MAXIMUM_LAG = 8
LAGS = 2 * MAXIMUM_LAG + 1
PIECE = 256
REACH = 384
LAG_ORDER = sorted(range(-MAXIMUM_LAG, MAXIMUM_LAG + 1), key=abs)
NEAR = 9
VMEM_LIMIT = 56 * 1024 * 1024


def band(row, half):
    wide = jnp.broadcast_to(row, (PIECE, REACH))
    return pltpu.roll(wide, 0, 1, stride=1, stride_axis=0).astype(jnp.bfloat16)


def normalize_kernel(half, taps_ref, x_ref, out_ref, src_ref, padded, level, filtered):
    parts, _, rows, channels = x_ref.shape
    samples = parts * rows
    tap_count = 2 * half + 1
    tail = padded.shape[0] - samples - half
    padded[:half] = jnp.zeros((half, channels), jnp.bfloat16)
    padded[half + samples :] = jnp.zeros((tail, channels), jnp.bfloat16)
    level[:half] = jnp.zeros((half, channels), jnp.bfloat16)
    level[half + samples :] = jnp.zeros((tail, channels), jnp.bfloat16)
    for i in range(parts):
        padded[half + i * rows : half + (i + 1) * rows] = x_ref[i, 0]
    taps = band(taps_ref[...], half)
    ones = jnp.where(
        lax.broadcasted_iota(jnp.int32, (1, REACH), 1) < tap_count, 1.0, 0.0
    ).astype(jnp.float32)
    box = band(ones, half)
    for p in range(samples // PIECE):
        low = p * PIECE
        value = jnp.dot(taps, padded[low : low + REACH], preferred_element_type=jnp.float32)
        filtered[low : low + PIECE] = value
        level[half + low : half + low + PIECE] = jnp.abs(value).astype(jnp.bfloat16)
    per = src_ref.shape[0]
    spacing = channels // per
    pick = (
        lax.broadcasted_iota(jnp.int32, (per, channels), 1)
        == spacing * lax.broadcasted_iota(jnp.int32, (per, channels), 0)
    )
    pick = jnp.where(pick, 1.0, 0.0).astype(jnp.bfloat16)
    for p in range(samples // PIECE):
        low = p * PIECE
        total = jnp.dot(box, level[low : low + REACH], preferred_element_type=jnp.float32)
        mean = total * (1.0 / tap_count)
        value = filtered[low : low + PIECE] / (mean + 1e-05)
        turned = jnp.transpose(value).astype(jnp.bfloat16)
        out_ref[:, low : low + PIECE] = turned
        src_ref[:, low : low + PIECE] = jnp.dot(
            pick, turned, preferred_element_type=jnp.float32
        ).astype(jnp.bfloat16)


def normalize(parts, taps):
    blocks, windows, rows, channels = parts.shape
    samples = blocks * rows
    half = (taps.shape[0] - 1) // 2
    sources = VIRTUAL_SOURCES // windows
    row = jnp.pad(taps.astype(jnp.float32), (0, REACH - taps.shape[0]))[None]
    return pl.pallas_call(
        functools.partial(normalize_kernel, half),
        grid=(windows,),
        out_shape=(
            jax.ShapeDtypeStruct((channels, windows * samples), jnp.bfloat16),
            jax.ShapeDtypeStruct((sources, windows * samples), jnp.bfloat16),
        ),
        in_specs=[
            pl.BlockSpec((1, REACH), lambda w: (0, 0)),
            pl.BlockSpec((blocks, 1, rows, channels), lambda w: (0, w, 0, 0)),
        ],
        out_specs=(
            pl.BlockSpec((channels, samples), lambda w: (0, w)),
            pl.BlockSpec((sources, samples), lambda w: (0, w)),
        ),
        scratch_shapes=[
            pltpu.VMEM((samples + REACH - PIECE, channels), jnp.bfloat16),
            pltpu.VMEM((samples + REACH - PIECE, channels), jnp.bfloat16),
            pltpu.VMEM((samples, channels), jnp.float32),
        ],
        compiler_params=pltpu.CompilerParams(vmem_limit_bytes=VMEM_LIMIT),
        name="normalize",
    )(row, parts)


def moved_rows(value, spot, lag):
    samples = value.shape[1]
    if lag == 0:
        return value
    kept = spot >= lag if lag > 0 else spot < samples + lag
    return jnp.where(kept, pltpu.roll(value, lag % samples, 1), 0.0)


def shift_kernel(x_ref, out_ref):
    rows, samples = x_ref.shape
    value = x_ref[...].astype(jnp.float32)
    spot = lax.broadcasted_iota(jnp.int32, (rows, samples), 1)
    for index, lag in enumerate(LAG_ORDER):
        out_ref[index] = moved_rows(value, spot, lag).astype(jnp.bfloat16)


def shift(receivers, windows):
    channels, length = receivers.shape
    samples = length // windows
    rows = min(32, channels)
    return pl.pallas_call(
        shift_kernel,
        grid=(channels // rows, windows),
        out_shape=jax.ShapeDtypeStruct((LAGS, channels, length), jnp.bfloat16),
        in_specs=[pl.BlockSpec((rows, samples), lambda c, w: (c, w))],
        out_specs=pl.BlockSpec((LAGS, rows, samples), lambda c, w: (0, c, w)),
        compiler_params=pltpu.CompilerParams(vmem_limit_bytes=VMEM_LIMIT),
        name="shift",
    )(receivers)


def other(line, here, k):
    far = (2 * here) // line
    near = here + far * (line - 1 - 2 * here)
    place = k + (k - near + line) // line
    return place + far * (line - 1 - 2 * place)


def gather_kernel(
    line, windows, src_ref, x_ref, out_ref, lagged_ref, held, local_sem, send_sem, recv_sem, out_sem
):
    chan, win = lax.axis_index("chan"), lax.axis_index("win")
    z, x, core = chan // 4, (chan // 2) % 2, chan % 2
    first_x = x + (1 - core) * (1 - 2 * x)
    first_win = win + core * (1 - 2 * win)
    second_x = x + core * (1 - 2 * x)
    second_win = win + (1 - core) * (1 - 2 * win)

    def device(z, x, core, win):
        return (z * 4 + x * 2 + core, win)

    def block(z, x, core, win):
        return (z * 4 + x * 2 + core) * 2 + win

    first = device(z, first_x, core, first_win)
    second = device(z, second_x, core, second_win)
    sibling = device(z, x, 1 - core, win)
    along = [device(other(line, z, k), x, core, win) for k in range(line - 1)]
    partners = [first, second, sibling] + along

    barrier = pltpu.get_barrier_semaphore()
    for partner in partners:
        pl.semaphore_signal(
            barrier, inc=1, device_id=partner, device_id_type=pl.DeviceIdType.MESH
        )
    pl.semaphore_wait(barrier, len(partners))

    started = []

    def send(target, number, own=False):
        copy = pltpu.make_async_remote_copy(
            src_ref=src_ref if own else out_ref.at[number],
            dst_ref=out_ref.at[number],
            send_sem=send_sem.at[len(started)],
            recv_sem=recv_sem.at[number],
            device_id=target,
            device_id_type=pl.DeviceIdType.MESH,
        )
        copy.start()
        started.append(copy)

    def arrived(number):
        pltpu.make_async_remote_copy(
            src_ref=out_ref.at[number],
            dst_ref=out_ref.at[number],
            send_sem=send_sem.at[0],
            recv_sem=recv_sem.at[number],
            device_id=sibling,
            device_id_type=pl.DeviceIdType.MESH,
        ).wait_recv()

    lags, rows, length = held.shape[1:]
    samples = length // windows
    chunks = x_ref.shape[0] // rows
    spot = lax.broadcasted_iota(jnp.int32, (rows, samples), 1)

    def write(slot, chunk):
        return pltpu.make_async_copy(
            held.at[slot],
            lagged_ref.at[:, pl.ds(pl.multiple_of(chunk * rows, rows), rows), :],
            out_sem.at[slot],
        )

    def shift_chunk(chunk, carry):
        slot = chunk % 2

        @pl.when(chunk >= 2)
        def _():
            write(slot, chunk - 2).wait()

        for w in range(windows):
            part = x_ref[
                pl.ds(pl.multiple_of(chunk * rows, rows), rows), w * samples : (w + 1) * samples
            ].astype(jnp.float32)
            for index, lag in enumerate(LAG_ORDER):
                held[slot, index, :, w * samples : (w + 1) * samples] = moved_rows(
                    part, spot, lag
                ).astype(jnp.bfloat16)
        write(slot, chunk).start()
        return carry

    own = block(z, x, core, win)
    mine = pltpu.make_async_copy(src_ref, out_ref.at[own], local_sem)
    for target in along + [first, second, sibling]:
        send(target, own, own=True)
    mine.start()
    steps = 4 * line
    done = 0
    for k in range(line):
        if k == 0:
            level = z
        else:
            level = other(line, z, k - 1)
            number = block(level, x, core, win)
            arrived(number)
            for target in (first, second, sibling):
                send(target, number)
        for step, (px, pwin) in enumerate(
            [(first_x, first_win), (second_x, second_win), (1 - x, 1 - win)]
        ):
            low, high = done, min(chunks, (done + 2))
            if high > low:
                lax.fori_loop(low, high, shift_chunk, 0)
                done = high
            number = block(level, px, core, pwin)
            arrived(number)
            if step == 0:
                send(second, number)
            send(sibling, number)
    if done < chunks:
        lax.fori_loop(done, chunks, shift_chunk, 0)
    for k in range(line):
        level = z if k == 0 else other(line, z, k - 1)
        for px, pwin in [(x, win), (first_x, first_win), (second_x, second_win), (1 - x, 1 - win)]:
            arrived(block(level, px, 1 - core, pwin))
    for chunk in range(max(0, chunks - 2), chunks):
        write(chunk % 2, chunk).wait()
    mine.wait()
    for copy in started:
        copy.wait_send()


def gather_and_shift(sources, receivers, blocks, windows):
    line = blocks // 4
    channels, length = receivers.shape
    rows = 16
    devices = blocks * windows
    whole = pl.BlockSpec(memory_space=pl.ANY)
    gathered, lagged = pl.pallas_call(
        functools.partial(gather_kernel, line, windows),
        out_shape=(
            jax.ShapeDtypeStruct((devices, *sources.shape), jnp.bfloat16),
            jax.ShapeDtypeStruct((LAGS, channels, length), jnp.bfloat16),
        ),
        in_specs=[whole, pl.BlockSpec(memory_space=pltpu.VMEM)],
        out_specs=(whole, whole),
        scratch_shapes=[
            pltpu.VMEM((2, LAGS, rows, length), jnp.bfloat16),
            pltpu.SemaphoreType.DMA,
            pltpu.SemaphoreType.DMA((devices - 1,)),
            pltpu.SemaphoreType.DMA((devices,)),
            pltpu.SemaphoreType.DMA((2,)),
        ],
        compiler_params=pltpu.CompilerParams(
            collective_id=0, has_side_effects=True, vmem_limit_bytes=VMEM_LIMIT
        ),
        name="gather_and_shift",
    )(sources, receivers)
    return gathered.reshape(blocks, VIRTUAL_SOURCES, length), lagged


def correlate_kernel(factor, partner, limit, lhs_ref, *refs):
    source_refs, out_ref = refs[:-1], refs[-1]
    slots = len(source_refs)
    _, rows, length = lhs_ref.shape

    def columns(index):
        low = (LAG_ORDER[index] + MAXIMUM_LAG) * VIRTUAL_SOURCES
        return slice(low, low + VIRTUAL_SOURCES)

    def multiply(group, low, high):
        panel = jnp.concatenate([source_refs[k][0] for k in group], axis=0)
        product = lax.dot_general(
            lhs_ref[low:high].reshape((high - low) * rows, length),
            panel,
            (((1,), (1,)), ((), ())),
            preferred_element_type=jnp.float32,
        )
        for index in range(low, high):
            for i, k in enumerate(group):
                piece = product[
                    (index - low) * rows : (index - low + 1) * rows,
                    i * VIRTUAL_SOURCES : (i + 1) * VIRTUAL_SOURCES,
                ]
                kept = abs(LAG_ORDER[index]) <= limit[k]
                out_ref[k, :, columns(index)] = jnp.where(kept, piece * factor, 0.0)

    def clear(group, low, high):
        for index in range(low, high):
            for k in group:
                out_ref[k, :, columns(index)] = jnp.zeros((rows, VIRTUAL_SOURCES), jnp.float32)

    for first in range(0, slots, 2):
        group = range(first, min(first + 2, slots))
        reach = functools.reduce(jnp.maximum, [limit[k] for k in group])
        for low, high in ((0, NEAR), (NEAR, LAGS)):
            needed = reach >= abs(LAG_ORDER[low])
            pl.when(needed)(functools.partial(multiply, group, low, high))
            pl.when(jnp.logical_not(needed))(functools.partial(clear, group, low, high))


def correlate(lagged, gathered, partner, limit):
    _, channels, length = lagged.shape
    slots = partner.shape[0]
    rows = min(64, channels)

    def source_spec(k):
        return pl.BlockSpec(
            (1, VIRTUAL_SOURCES, length), lambda c, partner, limit: (partner[k], 0, 0)
        )

    return pl.pallas_call(
        functools.partial(correlate_kernel, 1.0 / math.sqrt(length)),
        grid_spec=pltpu.PrefetchScalarGridSpec(
            num_scalar_prefetch=2,
            grid=(channels // rows,),
            in_specs=[pl.BlockSpec((LAGS, rows, length), lambda c, partner, limit: (0, c, 0))]
            + [source_spec(k) for k in range(slots)],
            out_specs=pl.BlockSpec(
                (slots, rows, LAGS * VIRTUAL_SOURCES), lambda c, partner, limit: (0, c, 0)
            ),
        ),
        out_shape=jax.ShapeDtypeStruct((slots, channels, LAGS * VIRTUAL_SOURCES), jnp.float32),
        compiler_params=pltpu.CompilerParams(vmem_limit_bytes=VMEM_LIMIT),
        name="correlate",
    )(partner, limit, lagged, *[gathered] * slots)


def gather_by_window(sources, partner, windows):
    samples = sources.shape[1] // windows
    blocks = lax.axis_size("chan")

    def one(window, panels):
        mine = lax.dynamic_slice_in_dim(sources, window * samples, samples, 1)
        mine = lax.all_gather(mine, "win", tiled=True)
        taken = lax.all_gather(mine, "chan")[partner]
        return lax.dynamic_update_slice_in_dim(panels, taken, window * samples, 2)

    empty = jnp.zeros((partner.shape[0], VIRTUAL_SOURCES, sources.shape[1]), sources.dtype)
    return lax.fori_loop(0, windows, one, empty)


def on_device(strain_rate, bandpass_taps, pair_offsets, lag_limit):
    blocks, windows = lax.axis_size("chan"), lax.axis_size("win")
    _, rows, total = strain_rate.shape
    channels = total // (blocks * windows)
    parts = lax.all_to_all(
        strain_rate[0], ("chan", "win"), split_axis=1, concat_axis=0, tiled=True
    ).reshape(blocks, windows, rows, channels)
    receivers, sources = normalize(parts, bandpass_taps)
    offsets = pair_offsets[0]
    used = offsets >= 0
    partner = jnp.where(used, (lax.axis_index("chan") + offsets) % blocks, 0).astype(jnp.int32)
    limit = jnp.where(used, lag_limit[0], -1).astype(jnp.int32)
    if windows > 2:
        lagged = shift(receivers, windows)
        panels = gather_by_window(sources, partner, windows)
        return correlate(lagged, panels, jnp.arange(partner.shape[0], dtype=jnp.int32), limit)
    gathered, lagged = gather_and_shift(sources, receivers, blocks, windows)
    return correlate(lagged, gathered, partner, limit)


def solution(mesh):
    placed = (P("win", "chan", None), P(), P("chan", None), P("chan", None))
    return jax.shard_map(
        on_device,
        mesh=mesh,
        in_specs=placed,
        out_specs=P(None, ("chan", "win"), None),
        check_vma=False,
    )
```

```python
import functools
import math

import jax
import jax.numpy as jnp
from jax import lax
from jax.experimental import pallas as pl
from jax.experimental.pallas import tpu as pltpu
from jax.sharding import PartitionSpec as P

VIRTUAL_SOURCES = 128
MAXIMUM_LAG = 8
LAGS = 2 * MAXIMUM_LAG + 1
PIECE = 256
REACH = 384
LAG_ORDER = sorted(range(-MAXIMUM_LAG, MAXIMUM_LAG + 1), key=abs)
NEAR = 9
VMEM_LIMIT = 56 * 1024 * 1024


def band(row, half):
    wide = jnp.broadcast_to(row, (PIECE, REACH))
    return pltpu.roll(wide, 0, 1, stride=1, stride_axis=0).astype(jnp.bfloat16)


def normalize_kernel(half, taps_ref, x_ref, out_ref, src_ref, padded, level, filtered):
    parts, _, rows, channels = x_ref.shape
    samples = parts * rows
    tap_count = 2 * half + 1
    tail = padded.shape[0] - samples - half
    padded[:half] = jnp.zeros((half, channels), jnp.bfloat16)
    padded[half + samples :] = jnp.zeros((tail, channels), jnp.bfloat16)
    level[:half] = jnp.zeros((half, channels), jnp.bfloat16)
    level[half + samples :] = jnp.zeros((tail, channels), jnp.bfloat16)
    for i in range(parts):
        padded[half + i * rows : half + (i + 1) * rows] = x_ref[i, 0]
    taps = band(taps_ref[...], half)
    ones = jnp.where(
        lax.broadcasted_iota(jnp.int32, (1, REACH), 1) < tap_count, 1.0, 0.0
    ).astype(jnp.float32)
    box = band(ones, half)
    for p in range(samples // PIECE):
        low = p * PIECE
        value = jnp.dot(taps, padded[low : low + REACH], preferred_element_type=jnp.float32)
        filtered[low : low + PIECE] = value
        level[half + low : half + low + PIECE] = jnp.abs(value).astype(jnp.bfloat16)
    per = src_ref.shape[0]
    spacing = channels // per
    pick = (
        lax.broadcasted_iota(jnp.int32, (per, channels), 1)
        == spacing * lax.broadcasted_iota(jnp.int32, (per, channels), 0)
    )
    pick = jnp.where(pick, 1.0, 0.0).astype(jnp.bfloat16)
    for p in range(samples // PIECE):
        low = p * PIECE
        total = jnp.dot(box, level[low : low + REACH], preferred_element_type=jnp.float32)
        mean = total * (1.0 / tap_count)
        value = filtered[low : low + PIECE] / (mean + 1e-05)
        turned = jnp.transpose(value).astype(jnp.bfloat16)
        out_ref[:, low : low + PIECE] = turned
        src_ref[:, low : low + PIECE] = jnp.dot(
            pick, turned, preferred_element_type=jnp.float32
        ).astype(jnp.bfloat16)


def normalize(parts, taps):
    blocks, windows, rows, channels = parts.shape
    samples = blocks * rows
    half = (taps.shape[0] - 1) // 2
    sources = VIRTUAL_SOURCES // windows
    row = jnp.pad(taps.astype(jnp.float32), (0, REACH - taps.shape[0]))[None]
    return pl.pallas_call(
        functools.partial(normalize_kernel, half),
        grid=(windows,),
        out_shape=(
            jax.ShapeDtypeStruct((channels, windows * samples), jnp.bfloat16),
            jax.ShapeDtypeStruct((sources, windows * samples), jnp.bfloat16),
        ),
        in_specs=[
            pl.BlockSpec((1, REACH), lambda w: (0, 0)),
            pl.BlockSpec((blocks, 1, rows, channels), lambda w: (0, w, 0, 0)),
        ],
        out_specs=(
            pl.BlockSpec((channels, samples), lambda w: (0, w)),
            pl.BlockSpec((sources, samples), lambda w: (0, w)),
        ),
        scratch_shapes=[
            pltpu.VMEM((samples + REACH - PIECE, channels), jnp.bfloat16),
            pltpu.VMEM((samples + REACH - PIECE, channels), jnp.bfloat16),
            pltpu.VMEM((samples, channels), jnp.float32),
        ],
        compiler_params=pltpu.CompilerParams(vmem_limit_bytes=VMEM_LIMIT),
        name="normalize",
    )(row, parts)


def moved_rows(value, spot, lag):
    samples = value.shape[1]
    if lag == 0:
        return value
    kept = spot >= lag if lag > 0 else spot < samples + lag
    return jnp.where(kept, pltpu.roll(value, lag % samples, 1), 0.0)


def shift_kernel(x_ref, out_ref):
    rows, samples = x_ref.shape
    value = x_ref[...].astype(jnp.float32)
    spot = lax.broadcasted_iota(jnp.int32, (rows, samples), 1)
    for index, lag in enumerate(LAG_ORDER):
        out_ref[index] = moved_rows(value, spot, lag).astype(jnp.bfloat16)


def shift(receivers, windows):
    channels, length = receivers.shape
    samples = length // windows
    rows = min(32, channels)
    return pl.pallas_call(
        shift_kernel,
        grid=(channels // rows, windows),
        out_shape=jax.ShapeDtypeStruct((LAGS, channels, length), jnp.bfloat16),
        in_specs=[pl.BlockSpec((rows, samples), lambda c, w: (c, w))],
        out_specs=pl.BlockSpec((LAGS, rows, samples), lambda c, w: (0, c, w)),
        compiler_params=pltpu.CompilerParams(vmem_limit_bytes=VMEM_LIMIT),
        name="shift",
    )(receivers)


def when(present, action):
    if present is None:
        action()
    else:
        pl.when(present)(action)


def gather_kernel(
    line, windows, src_ref, x_ref, out_ref, lagged_ref, held, local_sem, send_sem, recv_sem, out_sem
):
    chan, win = lax.axis_index("chan"), lax.axis_index("win")
    z, x, core = chan // 4, (chan // 2) % 2, chan % 2
    first_x = x + (1 - core) * (1 - 2 * x)
    first_win = win + core * (1 - 2 * win)
    second_x = x + core * (1 - 2 * x)
    second_win = win + (1 - core) * (1 - 2 * win)

    def device(z, x, core, win):
        return (z * 4 + x * 2 + core, win)

    def block(z, x, core, win):
        return (z * 4 + x * 2 + core) * 2 + win

    first = device(z, first_x, core, first_win)
    second = device(z, second_x, core, second_win)
    sibling = device(z, x, 1 - core, win)
    up, down = device(z + 1, x, core, win), device(z - 1, x, core, win)
    has_up, has_down = z + 1 < line, z >= 1

    barrier = pltpu.get_barrier_semaphore()

    def greet(partner):
        pl.semaphore_signal(
            barrier, inc=1, device_id=partner, device_id_type=pl.DeviceIdType.MESH
        )

    for partner in (first, second, sibling):
        greet(partner)
    when(has_up, functools.partial(greet, up))
    when(has_down, functools.partial(greet, down))
    levels_beside = (z + line - 1) // line + (2 * line - 2 - z) // line
    pl.semaphore_wait(barrier, 3 + levels_beside)

    started = []

    def send(target, number, present, own=False):
        copy = pltpu.make_async_remote_copy(
            src_ref=src_ref if own else out_ref.at[number],
            dst_ref=out_ref.at[number],
            send_sem=send_sem.at[len(started)],
            recv_sem=recv_sem.at[number],
            device_id=target,
            device_id_type=pl.DeviceIdType.MESH,
        )
        started.append((present, copy))
        when(present, copy.start)

    def arrived(number):
        pltpu.make_async_remote_copy(
            src_ref=out_ref.at[number],
            dst_ref=out_ref.at[number],
            send_sem=send_sem.at[0],
            recv_sem=recv_sem.at[number],
            device_id=sibling,
            device_id_type=pl.DeviceIdType.MESH,
        ).wait_recv()

    lags, rows, length = held.shape[1:]
    samples = length // windows
    chunks = x_ref.shape[0] // rows
    spot = lax.broadcasted_iota(jnp.int32, (rows, samples), 1)

    def write(slot, chunk):
        return pltpu.make_async_copy(
            held.at[slot],
            lagged_ref.at[:, pl.ds(pl.multiple_of(chunk * rows, rows), rows), :],
            out_sem.at[slot],
        )

    def shift_chunk(chunk, carry):
        slot = chunk % 2

        @pl.when(chunk >= 2)
        def _():
            write(slot, chunk - 2).wait()

        for w in range(windows):
            part = x_ref[
                pl.ds(pl.multiple_of(chunk * rows, rows), rows), w * samples : (w + 1) * samples
            ].astype(jnp.float32)
            for index, lag in enumerate(LAG_ORDER):
                held[slot, index, :, w * samples : (w + 1) * samples] = moved_rows(
                    part, spot, lag
                ).astype(jnp.bfloat16)
        write(slot, chunk).start()
        return carry

    own = block(z, x, core, win)
    mine = pltpu.make_async_copy(src_ref, out_ref.at[own], local_sem)
    send(up, own, has_up, own=True)
    send(down, own, has_down, own=True)
    for target in (first, second, sibling):
        send(target, own, None, own=True)
    mine.start()
    levels = [(z, None)]
    for r in range(1, line):
        levels += [(z - r, z >= r), (z + r, z + r < line)]
    done = 0
    for index, (level, present) in enumerate(levels):
        if index > 0:
            number = block(level, x, core, win)
            when(present, functools.partial(arrived, number))
            if index % 2 == 1:
                onward = jnp.logical_and(present, has_up)
                send(up, number, onward)
            else:
                onward = jnp.logical_and(present, has_down)
                send(down, number, onward)
            for target in (first, second, sibling):
                send(target, number, present)
        for step, (px, pwin) in enumerate(
            [(first_x, first_win), (second_x, second_win), (1 - x, 1 - win)]
        ):
            if done < chunks:
                lax.fori_loop(done, done + 1, shift_chunk, 0)
                done += 1
            number = block(level, px, core, pwin)
            when(present, functools.partial(arrived, number))
            if step == 0:
                send(second, number, present)
            send(sibling, number, present)
    if done < chunks:
        lax.fori_loop(done, chunks, shift_chunk, 0)
    for level in range(line):
        for px, pwin in [(x, win), (first_x, first_win), (second_x, second_win), (1 - x, 1 - win)]:
            arrived(block(level, px, 1 - core, pwin))
    for chunk in range(max(0, chunks - 2), chunks):
        write(chunk % 2, chunk).wait()
    mine.wait()
    for present, copy in started:
        when(present, copy.wait_send)


def gather_and_shift(sources, receivers, blocks, windows):
    line = blocks // 4
    channels, length = receivers.shape
    rows = 16
    devices = blocks * windows
    whole = pl.BlockSpec(memory_space=pl.ANY)
    gathered, lagged = pl.pallas_call(
        functools.partial(gather_kernel, line, windows),
        out_shape=(
            jax.ShapeDtypeStruct((devices, *sources.shape), jnp.bfloat16),
            jax.ShapeDtypeStruct((LAGS, channels, length), jnp.bfloat16),
        ),
        in_specs=[whole, pl.BlockSpec(memory_space=pltpu.VMEM)],
        out_specs=(whole, whole),
        scratch_shapes=[
            pltpu.VMEM((2, LAGS, rows, length), jnp.bfloat16),
            pltpu.SemaphoreType.DMA,
            pltpu.SemaphoreType.DMA((16 * line,)),
            pltpu.SemaphoreType.DMA((devices,)),
            pltpu.SemaphoreType.DMA((2,)),
        ],
        compiler_params=pltpu.CompilerParams(
            collective_id=0, has_side_effects=True, vmem_limit_bytes=VMEM_LIMIT
        ),
        name="gather_and_shift",
    )(sources, receivers)
    return gathered.reshape(blocks, VIRTUAL_SOURCES, length), lagged


def correlate_kernel(factor, partner, limit, lhs_ref, *refs):
    source_refs, out_ref = refs[:-1], refs[-1]
    slots = len(source_refs)
    _, rows, length = lhs_ref.shape

    def columns(index):
        low = (LAG_ORDER[index] + MAXIMUM_LAG) * VIRTUAL_SOURCES
        return slice(low, low + VIRTUAL_SOURCES)

    def multiply(group, low, high):
        panel = jnp.concatenate([source_refs[k][0] for k in group], axis=0)
        product = lax.dot_general(
            lhs_ref[low:high].reshape((high - low) * rows, length),
            panel,
            (((1,), (1,)), ((), ())),
            preferred_element_type=jnp.float32,
        )
        for index in range(low, high):
            for i, k in enumerate(group):
                piece = product[
                    (index - low) * rows : (index - low + 1) * rows,
                    i * VIRTUAL_SOURCES : (i + 1) * VIRTUAL_SOURCES,
                ]
                kept = abs(LAG_ORDER[index]) <= limit[k]
                out_ref[k, :, columns(index)] = jnp.where(kept, piece * factor, 0.0)

    def clear(group, low, high):
        for index in range(low, high):
            for k in group:
                out_ref[k, :, columns(index)] = jnp.zeros((rows, VIRTUAL_SOURCES), jnp.float32)

    for first in range(0, slots, 2):
        group = range(first, min(first + 2, slots))
        reach = functools.reduce(jnp.maximum, [limit[k] for k in group])
        for low, high in ((0, NEAR), (NEAR, LAGS)):
            needed = reach >= abs(LAG_ORDER[low])
            pl.when(needed)(functools.partial(multiply, group, low, high))
            pl.when(jnp.logical_not(needed))(functools.partial(clear, group, low, high))


def correlate(lagged, gathered, partner, limit):
    _, channels, length = lagged.shape
    slots = partner.shape[0]
    rows = min(64, channels)

    def source_spec(k):
        return pl.BlockSpec(
            (1, VIRTUAL_SOURCES, length), lambda c, partner, limit: (partner[k], 0, 0)
        )

    return pl.pallas_call(
        functools.partial(correlate_kernel, 1.0 / math.sqrt(length)),
        grid_spec=pltpu.PrefetchScalarGridSpec(
            num_scalar_prefetch=2,
            grid=(channels // rows,),
            in_specs=[pl.BlockSpec((LAGS, rows, length), lambda c, partner, limit: (0, c, 0))]
            + [source_spec(k) for k in range(slots)],
            out_specs=pl.BlockSpec(
                (slots, rows, LAGS * VIRTUAL_SOURCES), lambda c, partner, limit: (0, c, 0)
            ),
        ),
        out_shape=jax.ShapeDtypeStruct((slots, channels, LAGS * VIRTUAL_SOURCES), jnp.float32),
        compiler_params=pltpu.CompilerParams(vmem_limit_bytes=VMEM_LIMIT),
        name="correlate",
    )(partner, limit, lagged, *[gathered] * slots)


def gather_by_window(sources, partner, windows):
    samples = sources.shape[1] // windows
    blocks = lax.axis_size("chan")

    def one(window, panels):
        mine = lax.dynamic_slice_in_dim(sources, window * samples, samples, 1)
        mine = lax.all_gather(mine, "win", tiled=True)
        taken = lax.all_gather(mine, "chan")[partner]
        return lax.dynamic_update_slice_in_dim(panels, taken, window * samples, 2)

    empty = jnp.zeros((partner.shape[0], VIRTUAL_SOURCES, sources.shape[1]), sources.dtype)
    return lax.fori_loop(0, windows, one, empty)


def on_device(strain_rate, bandpass_taps, pair_offsets, lag_limit):
    blocks, windows = lax.axis_size("chan"), lax.axis_size("win")
    _, rows, total = strain_rate.shape
    channels = total // (blocks * windows)
    parts = lax.all_to_all(
        strain_rate[0], ("chan", "win"), split_axis=1, concat_axis=0, tiled=True
    ).reshape(blocks, windows, rows, channels)
    receivers, sources = normalize(parts, bandpass_taps)
    offsets = pair_offsets[0]
    used = offsets >= 0
    partner = jnp.where(used, (lax.axis_index("chan") + offsets) % blocks, 0).astype(jnp.int32)
    limit = jnp.where(used, lag_limit[0], -1).astype(jnp.int32)
    if windows > 2:
        lagged = shift(receivers, windows)
        panels = gather_by_window(sources, partner, windows)
        return correlate(lagged, panels, jnp.arange(partner.shape[0], dtype=jnp.int32), limit)
    gathered, lagged = gather_and_shift(sources, receivers, blocks, windows)
    return correlate(lagged, gathered, partner, limit)


def solution(mesh):
    placed = (P("win", "chan", None), P(), P("chan", None), P("chan", None))
    return jax.shard_map(
        on_device,
        mesh=mesh,
        in_specs=placed,
        out_specs=P(None, ("chan", "win"), None),
        check_vma=False,
    )
```

```python
import functools
import math

import jax
import jax.numpy as jnp
from jax import lax
from jax.experimental import pallas as pl
from jax.experimental.pallas import tpu as pltpu
from jax.sharding import PartitionSpec as P

VIRTUAL_SOURCES = 128
MAXIMUM_LAG = 8
LAGS = 2 * MAXIMUM_LAG + 1
PIECE = 256
REACH = 384
LAG_ORDER = sorted(range(-MAXIMUM_LAG, MAXIMUM_LAG + 1), key=abs)
NEAR = 9
VMEM_LIMIT = 56 * 1024 * 1024


def band(row, half):
    wide = jnp.broadcast_to(row, (PIECE, REACH))
    return pltpu.roll(wide, 0, 1, stride=1, stride_axis=0).astype(jnp.bfloat16)


def normalize_kernel(half, taps_ref, x_ref, out_ref, src_ref, padded, level, filtered):
    parts, _, rows, channels = x_ref.shape
    samples = parts * rows
    tap_count = 2 * half + 1
    tail = padded.shape[0] - samples - half
    padded[:half] = jnp.zeros((half, channels), jnp.bfloat16)
    padded[half + samples :] = jnp.zeros((tail, channels), jnp.bfloat16)
    level[:half] = jnp.zeros((half, channels), jnp.bfloat16)
    level[half + samples :] = jnp.zeros((tail, channels), jnp.bfloat16)
    for i in range(parts):
        padded[half + i * rows : half + (i + 1) * rows] = x_ref[i, 0]
    taps = band(taps_ref[...], half)
    ones = jnp.where(
        lax.broadcasted_iota(jnp.int32, (1, REACH), 1) < tap_count, 1.0, 0.0
    ).astype(jnp.float32)
    box = band(ones, half)
    for p in range(samples // PIECE):
        low = p * PIECE
        value = jnp.dot(taps, padded[low : low + REACH], preferred_element_type=jnp.float32)
        filtered[low : low + PIECE] = value
        level[half + low : half + low + PIECE] = jnp.abs(value).astype(jnp.bfloat16)
    per = src_ref.shape[0]
    spacing = channels // per
    pick = (
        lax.broadcasted_iota(jnp.int32, (per, channels), 1)
        == spacing * lax.broadcasted_iota(jnp.int32, (per, channels), 0)
    )
    pick = jnp.where(pick, 1.0, 0.0).astype(jnp.bfloat16)
    for p in range(samples // PIECE):
        low = p * PIECE
        total = jnp.dot(box, level[low : low + REACH], preferred_element_type=jnp.float32)
        mean = total * (1.0 / tap_count)
        value = filtered[low : low + PIECE] / (mean + 1e-05)
        turned = jnp.transpose(value).astype(jnp.bfloat16)
        out_ref[:, low : low + PIECE] = turned
        src_ref[:, low : low + PIECE] = jnp.dot(
            pick, turned, preferred_element_type=jnp.float32
        ).astype(jnp.bfloat16)


def normalize(parts, taps):
    blocks, windows, rows, channels = parts.shape
    samples = blocks * rows
    half = (taps.shape[0] - 1) // 2
    sources = VIRTUAL_SOURCES // windows
    row = jnp.pad(taps.astype(jnp.float32), (0, REACH - taps.shape[0]))[None]
    return pl.pallas_call(
        functools.partial(normalize_kernel, half),
        grid=(windows,),
        out_shape=(
            jax.ShapeDtypeStruct((channels, windows * samples), jnp.bfloat16),
            jax.ShapeDtypeStruct((sources, windows * samples), jnp.bfloat16),
        ),
        in_specs=[
            pl.BlockSpec((1, REACH), lambda w: (0, 0)),
            pl.BlockSpec((blocks, 1, rows, channels), lambda w: (0, w, 0, 0)),
        ],
        out_specs=(
            pl.BlockSpec((channels, samples), lambda w: (0, w)),
            pl.BlockSpec((sources, samples), lambda w: (0, w)),
        ),
        scratch_shapes=[
            pltpu.VMEM((samples + REACH - PIECE, channels), jnp.bfloat16),
            pltpu.VMEM((samples + REACH - PIECE, channels), jnp.bfloat16),
            pltpu.VMEM((samples, channels), jnp.float32),
        ],
        compiler_params=pltpu.CompilerParams(vmem_limit_bytes=VMEM_LIMIT),
        name="normalize",
    )(row, parts)


def moved_rows(value, spot, lag):
    samples = value.shape[1]
    if lag == 0:
        return value
    kept = spot >= lag if lag > 0 else spot < samples + lag
    return jnp.where(kept, pltpu.roll(value, lag % samples, 1), 0.0)


def shift_kernel(x_ref, out_ref):
    rows, samples = x_ref.shape
    value = x_ref[...].astype(jnp.float32)
    spot = lax.broadcasted_iota(jnp.int32, (rows, samples), 1)
    for index, lag in enumerate(LAG_ORDER):
        out_ref[index] = moved_rows(value, spot, lag).astype(jnp.bfloat16)


def shift(receivers, windows):
    channels, length = receivers.shape
    samples = length // windows
    rows = min(32, channels)
    return pl.pallas_call(
        shift_kernel,
        grid=(channels // rows, windows),
        out_shape=jax.ShapeDtypeStruct((LAGS, channels, length), jnp.bfloat16),
        in_specs=[pl.BlockSpec((rows, samples), lambda c, w: (c, w))],
        out_specs=pl.BlockSpec((LAGS, rows, samples), lambda c, w: (0, c, w)),
        compiler_params=pltpu.CompilerParams(vmem_limit_bytes=VMEM_LIMIT),
        name="shift",
    )(receivers)


def when(present, action):
    if present is None:
        action()
    else:
        pl.when(present)(action)


def gather_kernel(
    line, windows, src_ref, x_ref, out_ref, lagged_ref, held, local_sem, send_sem, recv_sem, out_sem
):
    chan, win = lax.axis_index("chan"), lax.axis_index("win")
    z, x, core = chan // 4, (chan // 2) % 2, chan % 2
    first_x = x + (1 - core) * (1 - 2 * x)
    first_win = win + core * (1 - 2 * win)
    second_x = x + core * (1 - 2 * x)
    second_win = win + (1 - core) * (1 - 2 * win)

    def device(z, x, core, win):
        return (z * 4 + x * 2 + core, win)

    def block(z, x, core, win):
        return (z * 4 + x * 2 + core) * 2 + win

    first = device(z, first_x, core, first_win)
    second = device(z, second_x, core, second_win)
    sibling = device(z, x, 1 - core, win)
    up, down = device(z + 1, x, core, win), device(z - 1, x, core, win)
    has_up, has_down = z + 1 < line, z >= 1

    barrier = pltpu.get_barrier_semaphore()

    def greet(partner):
        pl.semaphore_signal(
            barrier, inc=1, device_id=partner, device_id_type=pl.DeviceIdType.MESH
        )

    for partner in (first, second, sibling):
        greet(partner)
    when(has_up, functools.partial(greet, up))
    when(has_down, functools.partial(greet, down))
    levels_beside = (z + line - 1) // line + (2 * line - 2 - z) // line
    pl.semaphore_wait(barrier, 3 + levels_beside)

    started = []

    def send(target, number, present, own=False):
        copy = pltpu.make_async_remote_copy(
            src_ref=src_ref if own else out_ref.at[number],
            dst_ref=out_ref.at[number],
            send_sem=send_sem.at[len(started)],
            recv_sem=recv_sem.at[number],
            device_id=target,
            device_id_type=pl.DeviceIdType.MESH,
        )
        started.append((present, copy))
        when(present, copy.start)

    def arrived(number):
        pltpu.make_async_remote_copy(
            src_ref=out_ref.at[number],
            dst_ref=out_ref.at[number],
            send_sem=send_sem.at[0],
            recv_sem=recv_sem.at[number],
            device_id=sibling,
            device_id_type=pl.DeviceIdType.MESH,
        ).wait_recv()

    lags, rows, length = held.shape[1:]
    samples = length // windows
    chunks = x_ref.shape[0] // rows
    spot = lax.broadcasted_iota(jnp.int32, (rows, samples), 1)

    def write(slot, chunk):
        return pltpu.make_async_copy(
            held.at[slot],
            lagged_ref.at[:, pl.ds(pl.multiple_of(chunk * rows, rows), rows), :],
            out_sem.at[slot],
        )

    def shift_chunk(chunk, carry):
        slot = chunk % 2

        @pl.when(chunk >= 2)
        def _():
            write(slot, chunk - 2).wait()

        for w in range(windows):
            part = x_ref[
                pl.ds(pl.multiple_of(chunk * rows, rows), rows), w * samples : (w + 1) * samples
            ].astype(jnp.float32)
            for index, lag in enumerate(LAG_ORDER):
                held[slot, index, :, w * samples : (w + 1) * samples] = moved_rows(
                    part, spot, lag
                ).astype(jnp.bfloat16)
        write(slot, chunk).start()
        return carry

    own = block(z, x, core, win)
    mine = pltpu.make_async_copy(src_ref, out_ref.at[own], local_sem)
    send(up, own, has_up, own=True)
    send(down, own, has_down, own=True)
    for target in (first, second, sibling):
        send(target, own, None, own=True)
    mine.start()
    groups = [[(z, None, None, None)]]
    for r in range(1, line):
        groups.append([(z - r, z >= r, up, has_up), (z + r, z + r < line, down, has_down)])

    def from_level(group):
        for level, present, target, further in group:
            number = block(level, x, core, win)
            when(present, functools.partial(arrived, number))
            send(target, number, jnp.logical_and(present, further))
            for target in (first, second, sibling):
                send(target, number, present)

    def from_first(group):
        for level, present, _, _ in group:
            number = block(level, first_x, core, first_win)
            when(present, functools.partial(arrived, number))
            for target in (second, sibling):
                send(target, number, present)

    def from_second(group, px, pwin):
        for level, present, _, _ in group:
            number = block(level, px, core, pwin)
            when(present, functools.partial(arrived, number))
            send(sibling, number, present)

    share = chunks // (2 * line)
    done = 0
    for k in range(1, line + 2):
        if k < line:
            from_level(groups[k])
        if k <= line:
            lax.fori_loop(done, done + share, shift_chunk, 0)
            done += share
            from_first(groups[k - 1])
            lax.fori_loop(done, done + share, shift_chunk, 0)
            done += share
            from_second(groups[k - 1], second_x, second_win)
        if k >= 2:
            from_second(groups[k - 2], 1 - x, 1 - win)
    if done < chunks:
        lax.fori_loop(done, chunks, shift_chunk, 0)
    for level in range(line):
        for px, pwin in [(x, win), (first_x, first_win), (second_x, second_win), (1 - x, 1 - win)]:
            arrived(block(level, px, 1 - core, pwin))
    for chunk in range(max(0, chunks - 2), chunks):
        write(chunk % 2, chunk).wait()
    mine.wait()
    for present, copy in started:
        when(present, copy.wait_send)


def gather_and_shift(sources, receivers, blocks, windows):
    line = blocks // 4
    channels, length = receivers.shape
    rows = 16
    devices = blocks * windows
    whole = pl.BlockSpec(memory_space=pl.ANY)
    gathered, lagged = pl.pallas_call(
        functools.partial(gather_kernel, line, windows),
        out_shape=(
            jax.ShapeDtypeStruct((devices, *sources.shape), jnp.bfloat16),
            jax.ShapeDtypeStruct((LAGS, channels, length), jnp.bfloat16),
        ),
        in_specs=[whole, pl.BlockSpec(memory_space=pltpu.VMEM)],
        out_specs=(whole, whole),
        scratch_shapes=[
            pltpu.VMEM((2, LAGS, rows, length), jnp.bfloat16),
            pltpu.SemaphoreType.DMA,
            pltpu.SemaphoreType.DMA((16 * line,)),
            pltpu.SemaphoreType.DMA((devices,)),
            pltpu.SemaphoreType.DMA((2,)),
        ],
        compiler_params=pltpu.CompilerParams(
            collective_id=0, has_side_effects=True, vmem_limit_bytes=VMEM_LIMIT
        ),
        name="gather_and_shift",
    )(sources, receivers)
    return gathered.reshape(blocks, VIRTUAL_SOURCES, length), lagged


def correlate_kernel(factor, partner, limit, lhs_ref, *refs):
    source_refs, out_ref = refs[:-1], refs[-1]
    slots = len(source_refs)
    _, rows, length = lhs_ref.shape

    def columns(index):
        low = (LAG_ORDER[index] + MAXIMUM_LAG) * VIRTUAL_SOURCES
        return slice(low, low + VIRTUAL_SOURCES)

    def multiply(group, low, high):
        panel = jnp.concatenate([source_refs[k][0] for k in group], axis=0)
        product = lax.dot_general(
            lhs_ref[low:high].reshape((high - low) * rows, length),
            panel,
            (((1,), (1,)), ((), ())),
            preferred_element_type=jnp.float32,
        )
        for index in range(low, high):
            for i, k in enumerate(group):
                piece = product[
                    (index - low) * rows : (index - low + 1) * rows,
                    i * VIRTUAL_SOURCES : (i + 1) * VIRTUAL_SOURCES,
                ]
                kept = abs(LAG_ORDER[index]) <= limit[k]
                out_ref[k, :, columns(index)] = jnp.where(kept, piece * factor, 0.0)

    def clear(group, low, high):
        for index in range(low, high):
            for k in group:
                out_ref[k, :, columns(index)] = jnp.zeros((rows, VIRTUAL_SOURCES), jnp.float32)

    for first in range(0, slots, 2):
        group = range(first, min(first + 2, slots))
        reach = functools.reduce(jnp.maximum, [limit[k] for k in group])
        for low, high in ((0, NEAR), (NEAR, LAGS)):
            needed = reach >= abs(LAG_ORDER[low])
            pl.when(needed)(functools.partial(multiply, group, low, high))
            pl.when(jnp.logical_not(needed))(functools.partial(clear, group, low, high))


def correlate(lagged, gathered, partner, limit):
    _, channels, length = lagged.shape
    slots = partner.shape[0]
    rows = min(64, channels)

    def source_spec(k):
        return pl.BlockSpec(
            (1, VIRTUAL_SOURCES, length), lambda c, partner, limit: (partner[k], 0, 0)
        )

    return pl.pallas_call(
        functools.partial(correlate_kernel, 1.0 / math.sqrt(length)),
        grid_spec=pltpu.PrefetchScalarGridSpec(
            num_scalar_prefetch=2,
            grid=(channels // rows,),
            in_specs=[pl.BlockSpec((LAGS, rows, length), lambda c, partner, limit: (0, c, 0))]
            + [source_spec(k) for k in range(slots)],
            out_specs=pl.BlockSpec(
                (slots, rows, LAGS * VIRTUAL_SOURCES), lambda c, partner, limit: (0, c, 0)
            ),
        ),
        out_shape=jax.ShapeDtypeStruct((slots, channels, LAGS * VIRTUAL_SOURCES), jnp.float32),
        compiler_params=pltpu.CompilerParams(vmem_limit_bytes=VMEM_LIMIT),
        name="correlate",
    )(partner, limit, lagged, *[gathered] * slots)


def gather_by_window(sources, partner, windows):
    samples = sources.shape[1] // windows
    blocks = lax.axis_size("chan")

    def one(window, panels):
        mine = lax.dynamic_slice_in_dim(sources, window * samples, samples, 1)
        mine = lax.all_gather(mine, "win", tiled=True)
        taken = lax.all_gather(mine, "chan")[partner]
        return lax.dynamic_update_slice_in_dim(panels, taken, window * samples, 2)

    empty = jnp.zeros((partner.shape[0], VIRTUAL_SOURCES, sources.shape[1]), sources.dtype)
    return lax.fori_loop(0, windows, one, empty)


def on_device(strain_rate, bandpass_taps, pair_offsets, lag_limit):
    blocks, windows = lax.axis_size("chan"), lax.axis_size("win")
    _, rows, total = strain_rate.shape
    channels = total // (blocks * windows)
    parts = lax.all_to_all(
        strain_rate[0], ("chan", "win"), split_axis=1, concat_axis=0, tiled=True
    ).reshape(blocks, windows, rows, channels)
    receivers, sources = normalize(parts, bandpass_taps)
    offsets = pair_offsets[0]
    used = offsets >= 0
    partner = jnp.where(used, (lax.axis_index("chan") + offsets) % blocks, 0).astype(jnp.int32)
    limit = jnp.where(used, lag_limit[0], -1).astype(jnp.int32)
    if windows > 2:
        lagged = shift(receivers, windows)
        panels = gather_by_window(sources, partner, windows)
        return correlate(lagged, panels, jnp.arange(partner.shape[0], dtype=jnp.int32), limit)
    gathered, lagged = gather_and_shift(sources, receivers, blocks, windows)
    return correlate(lagged, gathered, partner, limit)


def solution(mesh):
    placed = (P("win", "chan", None), P(), P("chan", None), P("chan", None))
    return jax.shard_map(
        on_device,
        mesh=mesh,
        in_specs=placed,
        out_specs=P(None, ("chan", "win"), None),
        check_vma=False,
    )
```

```python
import functools
import math

import jax
import jax.numpy as jnp
from jax import lax
from jax.experimental import pallas as pl
from jax.experimental.pallas import tpu as pltpu
from jax.sharding import PartitionSpec as P

VIRTUAL_SOURCES = 128
MAXIMUM_LAG = 8
LAGS = 2 * MAXIMUM_LAG + 1
PIECE = 256
REACH = 384
LAG_ORDER = sorted(range(-MAXIMUM_LAG, MAXIMUM_LAG + 1), key=abs)
NEAR = 9
VMEM_LIMIT = 56 * 1024 * 1024


def band(row, half):
    wide = jnp.broadcast_to(row, (PIECE, REACH))
    return pltpu.roll(wide, 0, 1, stride=1, stride_axis=0).astype(jnp.bfloat16)


def clean(half, taps, box, parts, out_ref, src_ref, padded, level, filtered):
    rows, channels = parts[0].shape
    samples = len(parts) * rows
    tap_count = 2 * half + 1
    tail = padded.shape[0] - samples - half
    padded[:half] = jnp.zeros((half, channels), jnp.bfloat16)
    padded[half + samples :] = jnp.zeros((tail, channels), jnp.bfloat16)
    level[:half] = jnp.zeros((half, channels), jnp.bfloat16)
    level[half + samples :] = jnp.zeros((tail, channels), jnp.bfloat16)
    for i, part in enumerate(parts):
        padded[half + i * rows : half + (i + 1) * rows] = part[...]
    for p in range(samples // PIECE):
        low = p * PIECE
        value = jnp.dot(taps, padded[low : low + REACH], preferred_element_type=jnp.float32)
        filtered[low : low + PIECE] = value
        level[half + low : half + low + PIECE] = jnp.abs(value).astype(jnp.bfloat16)
    per = src_ref.shape[0]
    spacing = channels // per
    pick = (
        lax.broadcasted_iota(jnp.int32, (per, channels), 1)
        == spacing * lax.broadcasted_iota(jnp.int32, (per, channels), 0)
    )
    pick = jnp.where(pick, 1.0, 0.0).astype(jnp.bfloat16)
    for p in range(samples // PIECE):
        low = p * PIECE
        total = jnp.dot(box, level[low : low + REACH], preferred_element_type=jnp.float32)
        mean = total * (1.0 / tap_count)
        value = filtered[low : low + PIECE] / (mean + 1e-05)
        turned = jnp.transpose(value).astype(jnp.bfloat16)
        out_ref[:, low : low + PIECE] = turned
        src_ref[:, low : low + PIECE] = jnp.dot(
            pick, turned, preferred_element_type=jnp.float32
        ).astype(jnp.bfloat16)


def bands(half, taps_ref):
    ones = jnp.where(
        lax.broadcasted_iota(jnp.int32, (1, REACH), 1) < 2 * half + 1, 1.0, 0.0
    ).astype(jnp.float32)
    return band(taps_ref[...], half), band(ones, half)


def normalize_kernel(half, taps_ref, x_ref, out_ref, src_ref, padded, level, filtered):
    taps, box = bands(half, taps_ref)
    parts = [x_ref.at[i, 0] for i in range(x_ref.shape[0])]
    clean(half, taps, box, parts, out_ref, src_ref, padded, level, filtered)


def normalize(parts, taps):
    blocks, windows, rows, channels = parts.shape
    samples = blocks * rows
    half = (taps.shape[0] - 1) // 2
    sources = VIRTUAL_SOURCES // windows
    row = jnp.pad(taps.astype(jnp.float32), (0, REACH - taps.shape[0]))[None]
    return pl.pallas_call(
        functools.partial(normalize_kernel, half),
        grid=(windows,),
        out_shape=(
            jax.ShapeDtypeStruct((channels, windows * samples), jnp.bfloat16),
            jax.ShapeDtypeStruct((sources, windows * samples), jnp.bfloat16),
        ),
        in_specs=[
            pl.BlockSpec((1, REACH), lambda w: (0, 0)),
            pl.BlockSpec((blocks, 1, rows, channels), lambda w: (0, w, 0, 0)),
        ],
        out_specs=(
            pl.BlockSpec((channels, samples), lambda w: (0, w)),
            pl.BlockSpec((sources, samples), lambda w: (0, w)),
        ),
        scratch_shapes=[
            pltpu.VMEM((samples + REACH - PIECE, channels), jnp.bfloat16),
            pltpu.VMEM((samples + REACH - PIECE, channels), jnp.bfloat16),
            pltpu.VMEM((samples, channels), jnp.float32),
        ],
        compiler_params=pltpu.CompilerParams(vmem_limit_bytes=VMEM_LIMIT),
        name="normalize",
    )(row, parts)


def exchange_kernel(
    half, windows, taps_ref, x_ref, out_ref, src_ref, parts, padded, level, filtered, own_sem,
    send_sem, recv_sem
):
    chan, win = lax.axis_index("chan"), lax.axis_index("win")
    devices, rows, channels = parts.shape
    me = chan * windows + win

    def place(number):
        return (number // windows, number % windows)

    def copy(step):
        target = (me + step) % devices
        low = pl.multiple_of(target * channels, channels)
        return pltpu.make_async_remote_copy(
            src_ref=x_ref.at[:, pl.ds(low, channels)],
            dst_ref=parts.at[me],
            send_sem=send_sem.at[step],
            recv_sem=recv_sem.at[me],
            device_id=place(target),
            device_id_type=pl.DeviceIdType.MESH,
        )

    def greet(step, carry):
        pl.semaphore_signal(
            barrier,
            inc=1,
            device_id=place((me + step) % devices),
            device_id_type=pl.DeviceIdType.MESH,
        )
        return carry

    def start(step, carry):
        copy(step).start()
        return carry

    def arrive(step, carry):
        number = (me + step) % devices
        pltpu.make_async_remote_copy(
            src_ref=parts.at[number],
            dst_ref=parts.at[number],
            send_sem=send_sem.at[0],
            recv_sem=recv_sem.at[number],
            device_id=place(number),
            device_id_type=pl.DeviceIdType.MESH,
        ).wait_recv()
        return carry

    def leave(step, carry):
        copy(step).wait_send()
        return carry

    barrier = pltpu.get_barrier_semaphore()
    lax.fori_loop(1, devices, greet, 0)
    pl.semaphore_wait(barrier, devices - 1)
    lax.fori_loop(1, devices, start, 0)
    mine = pltpu.make_async_copy(
        x_ref.at[:, pl.ds(pl.multiple_of(me * channels, channels), channels)],
        parts.at[me],
        own_sem,
    )
    mine.start()
    taps, box = bands(half, taps_ref)
    mine.wait()
    lax.fori_loop(1, devices, arrive, 0)
    for w in range(windows):
        samples = devices // windows * rows
        along = pl.ds(w * samples, samples)
        clean(
            half,
            taps,
            box,
            [parts.at[i * windows + w] for i in range(devices // windows)],
            out_ref.at[:, along],
            src_ref.at[:, along],
            padded,
            level,
            filtered,
        )
    lax.fori_loop(1, devices, leave, 0)


def exchange_and_normalize(strain, taps, blocks, windows):
    devices = blocks * windows
    rows, total = strain.shape
    channels, samples = total // devices, blocks * rows
    half = (taps.shape[0] - 1) // 2
    sources = VIRTUAL_SOURCES // windows
    row = jnp.pad(taps.astype(jnp.float32), (0, REACH - taps.shape[0]))[None]
    vmem = pl.BlockSpec(memory_space=pltpu.VMEM)
    return pl.pallas_call(
        functools.partial(exchange_kernel, half, windows),
        out_shape=(
            jax.ShapeDtypeStruct((channels, windows * samples), jnp.bfloat16),
            jax.ShapeDtypeStruct((sources, windows * samples), jnp.bfloat16),
        ),
        in_specs=[vmem, pl.BlockSpec(memory_space=pl.ANY)],
        out_specs=(vmem, vmem),
        scratch_shapes=[
            pltpu.VMEM((devices, rows, channels), jnp.bfloat16),
            pltpu.VMEM((samples + REACH - PIECE, channels), jnp.bfloat16),
            pltpu.VMEM((samples + REACH - PIECE, channels), jnp.bfloat16),
            pltpu.VMEM((samples, channels), jnp.float32),
            pltpu.SemaphoreType.DMA,
            pltpu.SemaphoreType.DMA((devices,)),
            pltpu.SemaphoreType.DMA((devices,)),
        ],
        compiler_params=pltpu.CompilerParams(
            collective_id=1, has_side_effects=True, vmem_limit_bytes=VMEM_LIMIT
        ),
        name="exchange_and_normalize",
    )(row, strain)


def moved_rows(value, spot, lag):
    samples = value.shape[1]
    if lag == 0:
        return value
    kept = spot >= lag if lag > 0 else spot < samples + lag
    return jnp.where(kept, pltpu.roll(value, lag % samples, 1), 0.0)


def shift_kernel(x_ref, out_ref):
    rows, samples = x_ref.shape
    value = x_ref[...].astype(jnp.float32)
    spot = lax.broadcasted_iota(jnp.int32, (rows, samples), 1)
    for index, lag in enumerate(LAG_ORDER):
        out_ref[index] = moved_rows(value, spot, lag).astype(jnp.bfloat16)


def shift(receivers, windows):
    channels, length = receivers.shape
    samples = length // windows
    rows = min(32, channels)
    return pl.pallas_call(
        shift_kernel,
        grid=(channels // rows, windows),
        out_shape=jax.ShapeDtypeStruct((LAGS, channels, length), jnp.bfloat16),
        in_specs=[pl.BlockSpec((rows, samples), lambda c, w: (c, w))],
        out_specs=pl.BlockSpec((LAGS, rows, samples), lambda c, w: (0, c, w)),
        compiler_params=pltpu.CompilerParams(vmem_limit_bytes=VMEM_LIMIT),
        name="shift",
    )(receivers)


def when(present, action):
    if present is None:
        action()
    else:
        pl.when(present)(action)


def gather_kernel(
    line, windows, src_ref, x_ref, out_ref, lagged_ref, held, local_sem, send_sem, recv_sem, out_sem
):
    chan, win = lax.axis_index("chan"), lax.axis_index("win")
    z, x, core = chan // 4, (chan // 2) % 2, chan % 2
    first_x = x + (1 - core) * (1 - 2 * x)
    first_win = win + core * (1 - 2 * win)
    second_x = x + core * (1 - 2 * x)
    second_win = win + (1 - core) * (1 - 2 * win)

    def device(z, x, core, win):
        return (z * 4 + x * 2 + core, win)

    def block(z, x, core, win):
        return (z * 4 + x * 2 + core) * 2 + win

    first = device(z, first_x, core, first_win)
    second = device(z, second_x, core, second_win)
    sibling = device(z, x, 1 - core, win)
    up, down = device(z + 1, x, core, win), device(z - 1, x, core, win)
    has_up, has_down = z + 1 < line, z >= 1

    barrier = pltpu.get_barrier_semaphore()

    def greet(partner):
        pl.semaphore_signal(
            barrier, inc=1, device_id=partner, device_id_type=pl.DeviceIdType.MESH
        )

    for partner in (first, second, sibling):
        greet(partner)
    when(has_up, functools.partial(greet, up))
    when(has_down, functools.partial(greet, down))
    levels_beside = (z + line - 1) // line + (2 * line - 2 - z) // line
    pl.semaphore_wait(barrier, 3 + levels_beside)

    started = []

    def send(target, number, present, own=False):
        copy = pltpu.make_async_remote_copy(
            src_ref=src_ref if own else out_ref.at[number],
            dst_ref=out_ref.at[number],
            send_sem=send_sem.at[len(started)],
            recv_sem=recv_sem.at[number],
            device_id=target,
            device_id_type=pl.DeviceIdType.MESH,
        )
        started.append((present, copy))
        when(present, copy.start)

    def arrived(number):
        pltpu.make_async_remote_copy(
            src_ref=out_ref.at[number],
            dst_ref=out_ref.at[number],
            send_sem=send_sem.at[0],
            recv_sem=recv_sem.at[number],
            device_id=sibling,
            device_id_type=pl.DeviceIdType.MESH,
        ).wait_recv()

    lags, rows, length = held.shape[1:]
    samples = length // windows
    chunks = x_ref.shape[0] // rows
    spot = lax.broadcasted_iota(jnp.int32, (rows, samples), 1)

    def write(slot, chunk):
        return pltpu.make_async_copy(
            held.at[slot],
            lagged_ref.at[:, pl.ds(pl.multiple_of(chunk * rows, rows), rows), :],
            out_sem.at[slot],
        )

    def shift_chunk(chunk, carry):
        slot = chunk % 2

        @pl.when(chunk >= 2)
        def _():
            write(slot, chunk - 2).wait()

        for w in range(windows):
            part = x_ref[
                pl.ds(pl.multiple_of(chunk * rows, rows), rows), w * samples : (w + 1) * samples
            ].astype(jnp.float32)
            for index, lag in enumerate(LAG_ORDER):
                held[slot, index, :, w * samples : (w + 1) * samples] = moved_rows(
                    part, spot, lag
                ).astype(jnp.bfloat16)
        write(slot, chunk).start()
        return carry

    own = block(z, x, core, win)
    mine = pltpu.make_async_copy(src_ref, out_ref.at[own], local_sem)
    send(up, own, has_up, own=True)
    send(down, own, has_down, own=True)
    for target in (first, second, sibling):
        send(target, own, None, own=True)
    mine.start()
    groups = [[(z, None, None, None)]]
    for r in range(1, line):
        groups.append([(z - r, z >= r, up, has_up), (z + r, z + r < line, down, has_down)])

    def from_level(group):
        for level, present, target, further in group:
            number = block(level, x, core, win)
            when(present, functools.partial(arrived, number))
            send(target, number, jnp.logical_and(present, further))
            for target in (first, second, sibling):
                send(target, number, present)

    def from_first(group):
        for level, present, _, _ in group:
            number = block(level, first_x, core, first_win)
            when(present, functools.partial(arrived, number))
            for target in (second, sibling):
                send(target, number, present)

    def from_second(group, px, pwin):
        for level, present, _, _ in group:
            number = block(level, px, core, pwin)
            when(present, functools.partial(arrived, number))
            send(sibling, number, present)

    share = chunks // (2 * line)
    done = 0
    for k in range(1, line + 2):
        if k < line:
            from_level(groups[k])
        if k <= line:
            lax.fori_loop(done, done + share, shift_chunk, 0)
            done += share
            from_first(groups[k - 1])
            lax.fori_loop(done, done + share, shift_chunk, 0)
            done += share
            from_second(groups[k - 1], second_x, second_win)
        if k >= 2:
            from_second(groups[k - 2], 1 - x, 1 - win)
    if done < chunks:
        lax.fori_loop(done, chunks, shift_chunk, 0)
    for level in range(line):
        for px, pwin in [(x, win), (first_x, first_win), (second_x, second_win), (1 - x, 1 - win)]:
            arrived(block(level, px, 1 - core, pwin))
    for chunk in range(max(0, chunks - 2), chunks):
        write(chunk % 2, chunk).wait()
    mine.wait()
    for present, copy in started:
        when(present, copy.wait_send)


def gather_and_shift(sources, receivers, blocks, windows):
    line = blocks // 4
    channels, length = receivers.shape
    rows = 16
    devices = blocks * windows
    whole = pl.BlockSpec(memory_space=pl.ANY)
    gathered, lagged = pl.pallas_call(
        functools.partial(gather_kernel, line, windows),
        out_shape=(
            jax.ShapeDtypeStruct((devices, *sources.shape), jnp.bfloat16),
            jax.ShapeDtypeStruct((LAGS, channels, length), jnp.bfloat16),
        ),
        in_specs=[whole, pl.BlockSpec(memory_space=pltpu.VMEM)],
        out_specs=(whole, whole),
        scratch_shapes=[
            pltpu.VMEM((2, LAGS, rows, length), jnp.bfloat16),
            pltpu.SemaphoreType.DMA,
            pltpu.SemaphoreType.DMA((16 * line,)),
            pltpu.SemaphoreType.DMA((devices,)),
            pltpu.SemaphoreType.DMA((2,)),
        ],
        compiler_params=pltpu.CompilerParams(
            collective_id=0, has_side_effects=True, vmem_limit_bytes=VMEM_LIMIT
        ),
        name="gather_and_shift",
    )(sources, receivers)
    return gathered.reshape(blocks, VIRTUAL_SOURCES, length), lagged


def correlate_kernel(factor, partner, limit, lhs_ref, *refs):
    source_refs, out_ref = refs[:-1], refs[-1]
    slots = len(source_refs)
    _, rows, length = lhs_ref.shape

    def columns(index):
        low = (LAG_ORDER[index] + MAXIMUM_LAG) * VIRTUAL_SOURCES
        return slice(low, low + VIRTUAL_SOURCES)

    def multiply(group, low, high):
        panel = jnp.concatenate([source_refs[k][0] for k in group], axis=0)
        product = lax.dot_general(
            lhs_ref[low:high].reshape((high - low) * rows, length),
            panel,
            (((1,), (1,)), ((), ())),
            preferred_element_type=jnp.float32,
        )
        for index in range(low, high):
            for i, k in enumerate(group):
                piece = product[
                    (index - low) * rows : (index - low + 1) * rows,
                    i * VIRTUAL_SOURCES : (i + 1) * VIRTUAL_SOURCES,
                ]
                kept = abs(LAG_ORDER[index]) <= limit[k]
                out_ref[k, :, columns(index)] = jnp.where(kept, piece * factor, 0.0)

    def clear(group, low, high):
        for index in range(low, high):
            for k in group:
                out_ref[k, :, columns(index)] = jnp.zeros((rows, VIRTUAL_SOURCES), jnp.float32)

    for first in range(0, slots, 2):
        group = range(first, min(first + 2, slots))
        reach = functools.reduce(jnp.maximum, [limit[k] for k in group])
        for low, high in ((0, NEAR), (NEAR, LAGS)):
            needed = reach >= abs(LAG_ORDER[low])
            pl.when(needed)(functools.partial(multiply, group, low, high))
            pl.when(jnp.logical_not(needed))(functools.partial(clear, group, low, high))


def correlate(lagged, gathered, partner, limit):
    _, channels, length = lagged.shape
    slots = partner.shape[0]
    rows = min(64, channels)

    def source_spec(k):
        return pl.BlockSpec(
            (1, VIRTUAL_SOURCES, length), lambda c, partner, limit: (partner[k], 0, 0)
        )

    return pl.pallas_call(
        functools.partial(correlate_kernel, 1.0 / math.sqrt(length)),
        grid_spec=pltpu.PrefetchScalarGridSpec(
            num_scalar_prefetch=2,
            grid=(channels // rows,),
            in_specs=[pl.BlockSpec((LAGS, rows, length), lambda c, partner, limit: (0, c, 0))]
            + [source_spec(k) for k in range(slots)],
            out_specs=pl.BlockSpec(
                (slots, rows, LAGS * VIRTUAL_SOURCES), lambda c, partner, limit: (0, c, 0)
            ),
        ),
        out_shape=jax.ShapeDtypeStruct((slots, channels, LAGS * VIRTUAL_SOURCES), jnp.float32),
        compiler_params=pltpu.CompilerParams(vmem_limit_bytes=VMEM_LIMIT),
        name="correlate",
    )(partner, limit, lagged, *[gathered] * slots)


def gather_by_window(sources, partner, windows):
    samples = sources.shape[1] // windows
    blocks = lax.axis_size("chan")

    def one(window, panels):
        mine = lax.dynamic_slice_in_dim(sources, window * samples, samples, 1)
        mine = lax.all_gather(mine, "win", tiled=True)
        taken = lax.all_gather(mine, "chan")[partner]
        return lax.dynamic_update_slice_in_dim(panels, taken, window * samples, 2)

    empty = jnp.zeros((partner.shape[0], VIRTUAL_SOURCES, sources.shape[1]), sources.dtype)
    return lax.fori_loop(0, windows, one, empty)


def on_device(strain_rate, bandpass_taps, pair_offsets, lag_limit):
    blocks, windows = lax.axis_size("chan"), lax.axis_size("win")
    _, rows, total = strain_rate.shape
    channels = total // (blocks * windows)
    if windows > 2:
        parts = lax.all_to_all(
            strain_rate[0], ("chan", "win"), split_axis=1, concat_axis=0, tiled=True
        ).reshape(blocks, windows, rows, channels)
        receivers, sources = normalize(parts, bandpass_taps)
    else:
        receivers, sources = exchange_and_normalize(
            strain_rate[0], bandpass_taps, blocks, windows
        )
    offsets = pair_offsets[0]
    used = offsets >= 0
    partner = jnp.where(used, (lax.axis_index("chan") + offsets) % blocks, 0).astype(jnp.int32)
    limit = jnp.where(used, lag_limit[0], -1).astype(jnp.int32)
    if windows > 2:
        lagged = shift(receivers, windows)
        panels = gather_by_window(sources, partner, windows)
        return correlate(lagged, panels, jnp.arange(partner.shape[0], dtype=jnp.int32), limit)
    gathered, lagged = gather_and_shift(sources, receivers, blocks, windows)
    return correlate(lagged, gathered, partner, limit)


def solution(mesh):
    placed = (P("win", "chan", None), P(), P("chan", None), P("chan", None))
    return jax.shard_map(
        on_device,
        mesh=mesh,
        in_specs=placed,
        out_specs=P(None, ("chan", "win"), None),
        check_vma=False,
    )
```

```python
import functools
import math

import jax
import jax.numpy as jnp
from jax import lax
from jax.experimental import pallas as pl
from jax.experimental.pallas import tpu as pltpu
from jax.sharding import PartitionSpec as P

VIRTUAL_SOURCES = 128
MAXIMUM_LAG = 8
LAGS = 2 * MAXIMUM_LAG + 1
PIECE = 256
REACH = 384
LAG_ORDER = sorted(range(-MAXIMUM_LAG, MAXIMUM_LAG + 1), key=abs)
NEAR = 9
VMEM_LIMIT = 56 * 1024 * 1024


def band(row, half):
    wide = jnp.broadcast_to(row, (PIECE, REACH))
    return pltpu.roll(wide, 0, 1, stride=1, stride_axis=0).astype(jnp.bfloat16)


def clean(half, taps, box, parts, out_ref, src_ref, padded, level, filtered):
    rows, channels = parts[0].shape
    samples = len(parts) * rows
    tap_count = 2 * half + 1
    tail = padded.shape[0] - samples - half
    padded[:half] = jnp.zeros((half, channels), jnp.bfloat16)
    padded[half + samples :] = jnp.zeros((tail, channels), jnp.bfloat16)
    level[:half] = jnp.zeros((half, channels), jnp.bfloat16)
    level[half + samples :] = jnp.zeros((tail, channels), jnp.bfloat16)
    for i, part in enumerate(parts):
        padded[half + i * rows : half + (i + 1) * rows] = part[...]
    for p in range(samples // PIECE):
        low = p * PIECE
        value = jnp.dot(taps, padded[low : low + REACH], preferred_element_type=jnp.float32)
        filtered[low : low + PIECE] = value
        level[half + low : half + low + PIECE] = jnp.abs(value).astype(jnp.bfloat16)
    per = src_ref.shape[0]
    spacing = channels // per
    pick = (
        lax.broadcasted_iota(jnp.int32, (per, channels), 1)
        == spacing * lax.broadcasted_iota(jnp.int32, (per, channels), 0)
    )
    pick = jnp.where(pick, 1.0, 0.0).astype(jnp.bfloat16)
    for p in range(samples // PIECE):
        low = p * PIECE
        total = jnp.dot(box, level[low : low + REACH], preferred_element_type=jnp.float32)
        mean = total * (1.0 / tap_count)
        value = filtered[low : low + PIECE] / (mean + 1e-05)
        turned = jnp.transpose(value).astype(jnp.bfloat16)
        out_ref[:, low : low + PIECE] = turned
        src_ref[:, low : low + PIECE] = jnp.dot(
            pick, turned, preferred_element_type=jnp.float32
        ).astype(jnp.bfloat16)


def bands(half, taps_ref):
    ones = jnp.where(
        lax.broadcasted_iota(jnp.int32, (1, REACH), 1) < 2 * half + 1, 1.0, 0.0
    ).astype(jnp.float32)
    return band(taps_ref[...], half), band(ones, half)


def normalize_kernel(half, taps_ref, x_ref, out_ref, src_ref, padded, level, filtered):
    taps, box = bands(half, taps_ref)
    parts = [x_ref.at[i, 0] for i in range(x_ref.shape[0])]
    clean(half, taps, box, parts, out_ref, src_ref, padded, level, filtered)


def normalize(parts, taps):
    blocks, windows, rows, channels = parts.shape
    samples = blocks * rows
    half = (taps.shape[0] - 1) // 2
    sources = VIRTUAL_SOURCES // windows
    row = jnp.pad(taps.astype(jnp.float32), (0, REACH - taps.shape[0]))[None]
    return pl.pallas_call(
        functools.partial(normalize_kernel, half),
        grid=(windows,),
        out_shape=(
            jax.ShapeDtypeStruct((channels, windows * samples), jnp.bfloat16),
            jax.ShapeDtypeStruct((sources, windows * samples), jnp.bfloat16),
        ),
        in_specs=[
            pl.BlockSpec((1, REACH), lambda w: (0, 0)),
            pl.BlockSpec((blocks, 1, rows, channels), lambda w: (0, w, 0, 0)),
        ],
        out_specs=(
            pl.BlockSpec((channels, samples), lambda w: (0, w)),
            pl.BlockSpec((sources, samples), lambda w: (0, w)),
        ),
        scratch_shapes=[
            pltpu.VMEM((samples + REACH - PIECE, channels), jnp.bfloat16),
            pltpu.VMEM((samples + REACH - PIECE, channels), jnp.bfloat16),
            pltpu.VMEM((samples, channels), jnp.float32),
        ],
        compiler_params=pltpu.CompilerParams(vmem_limit_bytes=VMEM_LIMIT),
        name="normalize",
    )(row, parts)


def exchange_kernel(
    half, windows, taps_ref, x_ref, out_ref, src_ref, parts, padded, level, filtered, own_sem,
    send_sem, recv_sem
):
    chan, win = lax.axis_index("chan"), lax.axis_index("win")
    devices, rows, channels = parts.shape
    me = chan * windows + win

    def place(number):
        return (number // windows, number % windows)

    def copy(step):
        target = (me + step) % devices
        low = pl.multiple_of(target * channels, channels)
        return pltpu.make_async_remote_copy(
            src_ref=x_ref.at[:, pl.ds(low, channels)],
            dst_ref=parts.at[me],
            send_sem=send_sem.at[step],
            recv_sem=recv_sem.at[me],
            device_id=place(target),
            device_id_type=pl.DeviceIdType.MESH,
        )

    def greet(step, carry):
        pl.semaphore_signal(
            barrier,
            inc=1,
            device_id=place((me + step) % devices),
            device_id_type=pl.DeviceIdType.MESH,
        )
        return carry

    def start(step, carry):
        copy(step).start()
        return carry

    def arrive(step, carry):
        number = (me + step) % devices
        pltpu.make_async_remote_copy(
            src_ref=parts.at[number],
            dst_ref=parts.at[number],
            send_sem=send_sem.at[0],
            recv_sem=recv_sem.at[number],
            device_id=place(number),
            device_id_type=pl.DeviceIdType.MESH,
        ).wait_recv()
        return carry

    def leave(step, carry):
        copy(step).wait_send()
        return carry

    barrier = pltpu.get_barrier_semaphore()
    lax.fori_loop(1, devices, greet, 0)
    pl.semaphore_wait(barrier, devices - 1)
    lax.fori_loop(1, devices, start, 0)
    mine = pltpu.make_async_copy(
        x_ref.at[:, pl.ds(pl.multiple_of(me * channels, channels), channels)],
        parts.at[me],
        own_sem,
    )
    mine.start()
    taps, box = bands(half, taps_ref)
    mine.wait()
    lax.fori_loop(1, devices, arrive, 0)
    for w in range(windows):
        samples = devices // windows * rows
        along = pl.ds(w * samples, samples)
        clean(
            half,
            taps,
            box,
            [parts.at[i * windows + w] for i in range(devices // windows)],
            out_ref.at[:, along],
            src_ref.at[:, along],
            padded,
            level,
            filtered,
        )
    lax.fori_loop(1, devices, leave, 0)


def exchange_and_normalize(strain, taps, blocks, windows):
    devices = blocks * windows
    rows, total = strain.shape
    channels, samples = total // devices, blocks * rows
    half = (taps.shape[0] - 1) // 2
    sources = VIRTUAL_SOURCES // windows
    row = jnp.pad(taps.astype(jnp.float32), (0, REACH - taps.shape[0]))[None]
    vmem = pl.BlockSpec(memory_space=pltpu.VMEM)
    return pl.pallas_call(
        functools.partial(exchange_kernel, half, windows),
        out_shape=(
            jax.ShapeDtypeStruct((channels, windows * samples), jnp.bfloat16),
            jax.ShapeDtypeStruct((sources, windows * samples), jnp.bfloat16),
        ),
        in_specs=[vmem, pl.BlockSpec(memory_space=pl.ANY)],
        out_specs=(vmem, vmem),
        scratch_shapes=[
            pltpu.VMEM((devices, rows, channels), jnp.bfloat16),
            pltpu.VMEM((samples + REACH - PIECE, channels), jnp.bfloat16),
            pltpu.VMEM((samples + REACH - PIECE, channels), jnp.bfloat16),
            pltpu.VMEM((samples, channels), jnp.float32),
            pltpu.SemaphoreType.DMA,
            pltpu.SemaphoreType.DMA((devices,)),
            pltpu.SemaphoreType.DMA((devices,)),
        ],
        compiler_params=pltpu.CompilerParams(
            collective_id=1, has_side_effects=True, vmem_limit_bytes=16 * 1024 * 1024
        ),
        name="exchange_and_normalize",
    )(row, strain)


def moved_rows(value, spot, lag):
    samples = value.shape[1]
    if lag == 0:
        return value
    kept = spot >= lag if lag > 0 else spot < samples + lag
    return jnp.where(kept, pltpu.roll(value, lag % samples, 1), 0.0)


def shift_kernel(x_ref, out_ref):
    rows, samples = x_ref.shape
    value = x_ref[...].astype(jnp.float32)
    spot = lax.broadcasted_iota(jnp.int32, (rows, samples), 1)
    for index, lag in enumerate(LAG_ORDER):
        out_ref[index] = moved_rows(value, spot, lag).astype(jnp.bfloat16)


def shift(receivers, windows):
    channels, length = receivers.shape
    samples = length // windows
    rows = min(32, channels)
    return pl.pallas_call(
        shift_kernel,
        grid=(channels // rows, windows),
        out_shape=jax.ShapeDtypeStruct((LAGS, channels, length), jnp.bfloat16),
        in_specs=[pl.BlockSpec((rows, samples), lambda c, w: (c, w))],
        out_specs=pl.BlockSpec((LAGS, rows, samples), lambda c, w: (0, c, w)),
        compiler_params=pltpu.CompilerParams(vmem_limit_bytes=VMEM_LIMIT),
        name="shift",
    )(receivers)


def when(present, action):
    if present is None:
        action()
    else:
        pl.when(present)(action)


def gather_kernel(
    line, windows, src_ref, x_ref, out_ref, lagged_ref, held, local_sem, send_sem, recv_sem, out_sem
):
    chan, win = lax.axis_index("chan"), lax.axis_index("win")
    z, x, core = chan // 4, (chan // 2) % 2, chan % 2
    first_x = x + (1 - core) * (1 - 2 * x)
    first_win = win + core * (1 - 2 * win)
    second_x = x + core * (1 - 2 * x)
    second_win = win + (1 - core) * (1 - 2 * win)

    def device(z, x, core, win):
        return (z * 4 + x * 2 + core, win)

    def block(z, x, core, win):
        return (z * 4 + x * 2 + core) * 2 + win

    first = device(z, first_x, core, first_win)
    second = device(z, second_x, core, second_win)
    sibling = device(z, x, 1 - core, win)
    up, down = device(z + 1, x, core, win), device(z - 1, x, core, win)
    has_up, has_down = z + 1 < line, z >= 1

    barrier = pltpu.get_barrier_semaphore()

    def greet(partner):
        pl.semaphore_signal(
            barrier, inc=1, device_id=partner, device_id_type=pl.DeviceIdType.MESH
        )

    for partner in (first, second, sibling):
        greet(partner)
    when(has_up, functools.partial(greet, up))
    when(has_down, functools.partial(greet, down))
    levels_beside = (z + line - 1) // line + (2 * line - 2 - z) // line
    pl.semaphore_wait(barrier, 3 + levels_beside)

    started = []

    def send(target, number, present, own=False):
        copy = pltpu.make_async_remote_copy(
            src_ref=src_ref if own else out_ref.at[number],
            dst_ref=out_ref.at[number],
            send_sem=send_sem.at[len(started)],
            recv_sem=recv_sem.at[number],
            device_id=target,
            device_id_type=pl.DeviceIdType.MESH,
        )
        started.append((present, copy))
        when(present, copy.start)

    def arrived(number):
        pltpu.make_async_remote_copy(
            src_ref=out_ref.at[number],
            dst_ref=out_ref.at[number],
            send_sem=send_sem.at[0],
            recv_sem=recv_sem.at[number],
            device_id=sibling,
            device_id_type=pl.DeviceIdType.MESH,
        ).wait_recv()

    lags, rows, length = held.shape[1:]
    samples = length // windows
    chunks = x_ref.shape[0] // rows
    spot = lax.broadcasted_iota(jnp.int32, (rows, samples), 1)

    def write(slot, chunk):
        return pltpu.make_async_copy(
            held.at[slot],
            lagged_ref.at[:, pl.ds(pl.multiple_of(chunk * rows, rows), rows), :],
            out_sem.at[slot],
        )

    def shift_chunk(chunk, carry):
        slot = chunk % 2

        @pl.when(chunk >= 2)
        def _():
            write(slot, chunk - 2).wait()

        for w in range(windows):
            part = x_ref[
                pl.ds(pl.multiple_of(chunk * rows, rows), rows), w * samples : (w + 1) * samples
            ].astype(jnp.float32)
            for index, lag in enumerate(LAG_ORDER):
                held[slot, index, :, w * samples : (w + 1) * samples] = moved_rows(
                    part, spot, lag
                ).astype(jnp.bfloat16)
        write(slot, chunk).start()
        return carry

    own = block(z, x, core, win)
    mine = pltpu.make_async_copy(src_ref, out_ref.at[own], local_sem)
    send(up, own, has_up, own=True)
    send(down, own, has_down, own=True)
    for target in (first, second, sibling):
        send(target, own, None, own=True)
    mine.start()
    groups = [[(z, None, None, None)]]
    for r in range(1, line):
        groups.append([(z - r, z >= r, up, has_up), (z + r, z + r < line, down, has_down)])

    def from_level(group):
        for level, present, target, further in group:
            number = block(level, x, core, win)
            when(present, functools.partial(arrived, number))
            send(target, number, jnp.logical_and(present, further))
            for target in (first, second, sibling):
                send(target, number, present)

    def from_first(group):
        for level, present, _, _ in group:
            number = block(level, first_x, core, first_win)
            when(present, functools.partial(arrived, number))
            for target in (second, sibling):
                send(target, number, present)

    def from_second(group, px, pwin):
        for level, present, _, _ in group:
            number = block(level, px, core, pwin)
            when(present, functools.partial(arrived, number))
            send(sibling, number, present)

    share = chunks // (2 * line)
    done = 0
    for k in range(1, line + 2):
        if k < line:
            from_level(groups[k])
        if k <= line:
            lax.fori_loop(done, done + share, shift_chunk, 0)
            done += share
            from_first(groups[k - 1])
            lax.fori_loop(done, done + share, shift_chunk, 0)
            done += share
            from_second(groups[k - 1], second_x, second_win)
        if k >= 2:
            from_second(groups[k - 2], 1 - x, 1 - win)
    if done < chunks:
        lax.fori_loop(done, chunks, shift_chunk, 0)
    for level in range(line):
        for px, pwin in [(x, win), (first_x, first_win), (second_x, second_win), (1 - x, 1 - win)]:
            arrived(block(level, px, 1 - core, pwin))
    for chunk in range(max(0, chunks - 2), chunks):
        write(chunk % 2, chunk).wait()
    mine.wait()
    for present, copy in started:
        when(present, copy.wait_send)


def gather_and_shift(sources, receivers, blocks, windows):
    line = blocks // 4
    channels, length = receivers.shape
    rows = 16
    devices = blocks * windows
    whole = pl.BlockSpec(memory_space=pl.ANY)
    gathered, lagged = pl.pallas_call(
        functools.partial(gather_kernel, line, windows),
        out_shape=(
            jax.ShapeDtypeStruct((devices, *sources.shape), jnp.bfloat16),
            jax.ShapeDtypeStruct((LAGS, channels, length), jnp.bfloat16),
        ),
        in_specs=[whole, pl.BlockSpec(memory_space=pltpu.VMEM)],
        out_specs=(whole, whole),
        scratch_shapes=[
            pltpu.VMEM((2, LAGS, rows, length), jnp.bfloat16),
            pltpu.SemaphoreType.DMA,
            pltpu.SemaphoreType.DMA((16 * line,)),
            pltpu.SemaphoreType.DMA((devices,)),
            pltpu.SemaphoreType.DMA((2,)),
        ],
        compiler_params=pltpu.CompilerParams(
            collective_id=0, has_side_effects=True, vmem_limit_bytes=12 * 1024 * 1024
        ),
        name="gather_and_shift",
    )(sources, receivers)
    return gathered.reshape(blocks, VIRTUAL_SOURCES, length), lagged


def correlate_kernel(factor, partner, limit, lhs_ref, *refs):
    source_refs, out_ref = refs[:-1], refs[-1]
    slots = len(source_refs)
    _, rows, length = lhs_ref.shape

    def columns(index):
        low = (LAG_ORDER[index] + MAXIMUM_LAG) * VIRTUAL_SOURCES
        return slice(low, low + VIRTUAL_SOURCES)

    def multiply(group, low, high):
        panel = jnp.concatenate([source_refs[k][0] for k in group], axis=0)
        product = lax.dot_general(
            lhs_ref[low:high].reshape((high - low) * rows, length),
            panel,
            (((1,), (1,)), ((), ())),
            preferred_element_type=jnp.float32,
        )
        for index in range(low, high):
            for i, k in enumerate(group):
                piece = product[
                    (index - low) * rows : (index - low + 1) * rows,
                    i * VIRTUAL_SOURCES : (i + 1) * VIRTUAL_SOURCES,
                ]
                kept = abs(LAG_ORDER[index]) <= limit[k]
                out_ref[k, :, columns(index)] = jnp.where(kept, piece * factor, 0.0)

    def clear(group, low, high):
        for index in range(low, high):
            for k in group:
                out_ref[k, :, columns(index)] = jnp.zeros((rows, VIRTUAL_SOURCES), jnp.float32)

    for first in range(0, slots, 2):
        group = range(first, min(first + 2, slots))
        reach = functools.reduce(jnp.maximum, [limit[k] for k in group])
        for low, high in ((0, NEAR), (NEAR, LAGS)):
            needed = reach >= abs(LAG_ORDER[low])
            pl.when(needed)(functools.partial(multiply, group, low, high))
            pl.when(jnp.logical_not(needed))(functools.partial(clear, group, low, high))


def correlate(lagged, gathered, partner, limit):
    _, channels, length = lagged.shape
    slots = partner.shape[0]
    rows = min(64, channels)
    held = 2 * length * (LAGS * rows + slots * VIRTUAL_SOURCES)
    held += 4 * slots * rows * LAGS * VIRTUAL_SOURCES
    limit_bytes = min(VMEM_LIMIT, 2 * held + 6 * 1024 * 1024)

    def source_spec(k):
        return pl.BlockSpec(
            (1, VIRTUAL_SOURCES, length), lambda c, partner, limit: (partner[k], 0, 0)
        )

    return pl.pallas_call(
        functools.partial(correlate_kernel, 1.0 / math.sqrt(length)),
        grid_spec=pltpu.PrefetchScalarGridSpec(
            num_scalar_prefetch=2,
            grid=(channels // rows,),
            in_specs=[pl.BlockSpec((LAGS, rows, length), lambda c, partner, limit: (0, c, 0))]
            + [source_spec(k) for k in range(slots)],
            out_specs=pl.BlockSpec(
                (slots, rows, LAGS * VIRTUAL_SOURCES), lambda c, partner, limit: (0, c, 0)
            ),
        ),
        out_shape=jax.ShapeDtypeStruct((slots, channels, LAGS * VIRTUAL_SOURCES), jnp.float32),
        compiler_params=pltpu.CompilerParams(vmem_limit_bytes=limit_bytes),
        name="correlate",
    )(partner, limit, lagged, *[gathered] * slots)


def gather_by_window(sources, partner, windows):
    samples = sources.shape[1] // windows
    blocks = lax.axis_size("chan")

    def one(window, panels):
        mine = lax.dynamic_slice_in_dim(sources, window * samples, samples, 1)
        mine = lax.all_gather(mine, "win", tiled=True)
        taken = lax.all_gather(mine, "chan")[partner]
        return lax.dynamic_update_slice_in_dim(panels, taken, window * samples, 2)

    empty = jnp.zeros((partner.shape[0], VIRTUAL_SOURCES, sources.shape[1]), sources.dtype)
    return lax.fori_loop(0, windows, one, empty)


def on_device(strain_rate, bandpass_taps, pair_offsets, lag_limit):
    blocks, windows = lax.axis_size("chan"), lax.axis_size("win")
    _, rows, total = strain_rate.shape
    channels = total // (blocks * windows)
    if windows > 2:
        parts = lax.all_to_all(
            strain_rate[0], ("chan", "win"), split_axis=1, concat_axis=0, tiled=True
        ).reshape(blocks, windows, rows, channels)
        receivers, sources = normalize(parts, bandpass_taps)
    else:
        receivers, sources = exchange_and_normalize(
            strain_rate[0], bandpass_taps, blocks, windows
        )
    offsets = pair_offsets[0]
    used = offsets >= 0
    partner = jnp.where(used, (lax.axis_index("chan") + offsets) % blocks, 0).astype(jnp.int32)
    limit = jnp.where(used, lag_limit[0], -1).astype(jnp.int32)
    if windows > 2:
        lagged = shift(receivers, windows)
        panels = gather_by_window(sources, partner, windows)
        return correlate(lagged, panels, jnp.arange(partner.shape[0], dtype=jnp.int32), limit)
    gathered, lagged = gather_and_shift(sources, receivers, blocks, windows)
    return correlate(lagged, gathered, partner, limit)


def solution(mesh):
    placed = (P("win", "chan", None), P(), P("chan", None), P("chan", None))
    return jax.shard_map(
        on_device,
        mesh=mesh,
        in_specs=placed,
        out_specs=P(None, ("chan", "win"), None),
        check_vma=False,
    )
```

```python
import functools
import itertools
import math

import jax
import jax.numpy as jnp
from jax import lax
from jax.experimental import pallas as pl
from jax.experimental.pallas import tpu as pltpu
from jax.sharding import PartitionSpec as P

VIRTUAL_SOURCES = 128
MAXIMUM_LAG = 8
LAGS = 2 * MAXIMUM_LAG + 1
PIECE = 256
REACH = 384
LAG_ORDER = sorted(range(-MAXIMUM_LAG, MAXIMUM_LAG + 1), key=abs)
NEAR = 9
HALVES = 2
VMEM_LIMIT = 56 * 1024 * 1024


def band(row, half):
    wide = jnp.broadcast_to(row, (PIECE, REACH))
    return pltpu.roll(wide, 0, 1, stride=1, stride_axis=0).astype(jnp.bfloat16)


def clean(half, taps, box, parts, out_ref, src_ref, padded, level, filtered):
    rows, channels = parts[0].shape
    samples = len(parts) * rows
    tap_count = 2 * half + 1
    tail = padded.shape[0] - samples - half
    padded[:half] = jnp.zeros((half, channels), jnp.bfloat16)
    padded[half + samples :] = jnp.zeros((tail, channels), jnp.bfloat16)
    level[:half] = jnp.zeros((half, channels), jnp.bfloat16)
    level[half + samples :] = jnp.zeros((tail, channels), jnp.bfloat16)
    for i, part in enumerate(parts):
        padded[half + i * rows : half + (i + 1) * rows] = part[...]
    for p in range(samples // PIECE):
        low = p * PIECE
        value = jnp.dot(taps, padded[low : low + REACH], preferred_element_type=jnp.float32)
        filtered[low : low + PIECE] = value
        level[half + low : half + low + PIECE] = jnp.abs(value).astype(jnp.bfloat16)
    per = src_ref.shape[0]
    spacing = channels // per
    pick = (
        lax.broadcasted_iota(jnp.int32, (per, channels), 1)
        == spacing * lax.broadcasted_iota(jnp.int32, (per, channels), 0)
    )
    pick = jnp.where(pick, 1.0, 0.0).astype(jnp.bfloat16)
    for p in range(samples // PIECE):
        low = p * PIECE
        total = jnp.dot(box, level[low : low + REACH], preferred_element_type=jnp.float32)
        mean = total * (1.0 / tap_count)
        value = filtered[low : low + PIECE] / (mean + 1e-05)
        turned = jnp.transpose(value).astype(jnp.bfloat16)
        out_ref[:, low : low + PIECE] = turned
        src_ref[:, low : low + PIECE] = jnp.dot(
            pick, turned, preferred_element_type=jnp.float32
        ).astype(jnp.bfloat16)


def bands(half, taps_ref):
    ones = jnp.where(
        lax.broadcasted_iota(jnp.int32, (1, REACH), 1) < 2 * half + 1, 1.0, 0.0
    ).astype(jnp.float32)
    return band(taps_ref[...], half), band(ones, half)


def normalize_kernel(half, taps_ref, x_ref, out_ref, src_ref, padded, level, filtered):
    taps, box = bands(half, taps_ref)
    parts = [x_ref.at[i, 0] for i in range(x_ref.shape[0])]
    clean(half, taps, box, parts, out_ref, src_ref, padded, level, filtered)


def normalize(parts, taps):
    blocks, windows, rows, channels = parts.shape
    samples = blocks * rows
    half = (taps.shape[0] - 1) // 2
    sources = VIRTUAL_SOURCES // windows
    row = jnp.pad(taps.astype(jnp.float32), (0, REACH - taps.shape[0]))[None]
    return pl.pallas_call(
        functools.partial(normalize_kernel, half),
        grid=(windows,),
        out_shape=(
            jax.ShapeDtypeStruct((channels, windows * samples), jnp.bfloat16),
            jax.ShapeDtypeStruct((sources, windows * samples), jnp.bfloat16),
        ),
        in_specs=[
            pl.BlockSpec((1, REACH), lambda w: (0, 0)),
            pl.BlockSpec((blocks, 1, rows, channels), lambda w: (0, w, 0, 0)),
        ],
        out_specs=(
            pl.BlockSpec((channels, samples), lambda w: (0, w)),
            pl.BlockSpec((sources, samples), lambda w: (0, w)),
        ),
        scratch_shapes=[
            pltpu.VMEM((samples + REACH - PIECE, channels), jnp.bfloat16),
            pltpu.VMEM((samples + REACH - PIECE, channels), jnp.bfloat16),
            pltpu.VMEM((samples, channels), jnp.float32),
        ],
        compiler_params=pltpu.CompilerParams(vmem_limit_bytes=VMEM_LIMIT),
        name="normalize",
    )(row, parts)


def exchange_kernel(
    half, windows, taps_ref, x_ref, out_ref, src_ref, parts, padded, level, filtered, own_sem,
    send_sem, recv_sem
):
    chan, win = lax.axis_index("chan"), lax.axis_index("win")
    devices, rows, channels = parts.shape
    me = chan * windows + win

    def place(number):
        return (number // windows, number % windows)

    def copy(step):
        target = (me + step) % devices
        low = pl.multiple_of(target * channels, channels)
        return pltpu.make_async_remote_copy(
            src_ref=x_ref.at[:, pl.ds(low, channels)],
            dst_ref=parts.at[me],
            send_sem=send_sem.at[step],
            recv_sem=recv_sem.at[me],
            device_id=place(target),
            device_id_type=pl.DeviceIdType.MESH,
        )

    def greet(step, carry):
        pl.semaphore_signal(
            barrier,
            inc=1,
            device_id=place((me + step) % devices),
            device_id_type=pl.DeviceIdType.MESH,
        )
        return carry

    def start(step, carry):
        copy(step).start()
        return carry

    def arrive(step, carry):
        number = (me + step) % devices
        pltpu.make_async_remote_copy(
            src_ref=parts.at[number],
            dst_ref=parts.at[number],
            send_sem=send_sem.at[0],
            recv_sem=recv_sem.at[number],
            device_id=place(number),
            device_id_type=pl.DeviceIdType.MESH,
        ).wait_recv()
        return carry

    def leave(step, carry):
        copy(step).wait_send()
        return carry

    barrier = pltpu.get_barrier_semaphore()
    lax.fori_loop(1, devices, greet, 0)
    pl.semaphore_wait(barrier, devices - 1)
    lax.fori_loop(1, devices, start, 0)
    mine = pltpu.make_async_copy(
        x_ref.at[:, pl.ds(pl.multiple_of(me * channels, channels), channels)],
        parts.at[me],
        own_sem,
    )
    mine.start()
    taps, box = bands(half, taps_ref)
    mine.wait()
    lax.fori_loop(1, devices, arrive, 0)
    for w in range(windows):
        samples = devices // windows * rows
        along = pl.ds(w * samples, samples)
        clean(
            half,
            taps,
            box,
            [parts.at[i * windows + w] for i in range(devices // windows)],
            out_ref.at[:, along],
            src_ref.at[:, along],
            padded,
            level,
            filtered,
        )
    lax.fori_loop(1, devices, leave, 0)


def exchange_and_normalize(strain, taps, blocks, windows):
    devices = blocks * windows
    rows, total = strain.shape
    channels, samples = total // devices, blocks * rows
    half = (taps.shape[0] - 1) // 2
    sources = VIRTUAL_SOURCES // windows
    row = jnp.pad(taps.astype(jnp.float32), (0, REACH - taps.shape[0]))[None]
    vmem = pl.BlockSpec(memory_space=pltpu.VMEM)
    return pl.pallas_call(
        functools.partial(exchange_kernel, half, windows),
        out_shape=(
            jax.ShapeDtypeStruct((channels, windows * samples), jnp.bfloat16),
            jax.ShapeDtypeStruct((sources, windows * samples), jnp.bfloat16),
        ),
        in_specs=[vmem, pl.BlockSpec(memory_space=pl.ANY)],
        out_specs=(vmem, vmem),
        scratch_shapes=[
            pltpu.VMEM((devices, rows, channels), jnp.bfloat16),
            pltpu.VMEM((samples + REACH - PIECE, channels), jnp.bfloat16),
            pltpu.VMEM((samples + REACH - PIECE, channels), jnp.bfloat16),
            pltpu.VMEM((samples, channels), jnp.float32),
            pltpu.SemaphoreType.DMA,
            pltpu.SemaphoreType.DMA((devices,)),
            pltpu.SemaphoreType.DMA((devices,)),
        ],
        compiler_params=pltpu.CompilerParams(
            collective_id=1, has_side_effects=True, vmem_limit_bytes=16 * 1024 * 1024
        ),
        name="exchange_and_normalize",
    )(row, strain)


def moved_rows(value, spot, lag):
    samples = value.shape[1]
    if lag == 0:
        return value
    kept = spot >= lag if lag > 0 else spot < samples + lag
    return jnp.where(kept, pltpu.roll(value, lag % samples, 1), 0.0)


def shift_kernel(x_ref, out_ref):
    rows, samples = x_ref.shape
    value = x_ref[...].astype(jnp.float32)
    spot = lax.broadcasted_iota(jnp.int32, (rows, samples), 1)
    for index, lag in enumerate(LAG_ORDER):
        out_ref[index] = moved_rows(value, spot, lag).astype(jnp.bfloat16)


def shift(receivers, windows):
    channels, length = receivers.shape
    samples = length // windows
    rows = min(32, channels)
    return pl.pallas_call(
        shift_kernel,
        grid=(channels // rows, windows),
        out_shape=jax.ShapeDtypeStruct((LAGS, channels, length), jnp.bfloat16),
        in_specs=[pl.BlockSpec((rows, samples), lambda c, w: (c, w))],
        out_specs=pl.BlockSpec((LAGS, rows, samples), lambda c, w: (0, c, w)),
        compiler_params=pltpu.CompilerParams(vmem_limit_bytes=VMEM_LIMIT),
        name="shift",
    )(receivers)


def when(present, action):
    if present is None:
        action()
    else:
        pl.when(present)(action)


def gather_kernel(
    line, windows, src_ref, x_ref, out_ref, lagged_ref, held, local_sem, send_sem, recv_sem, out_sem
):
    chan, win = lax.axis_index("chan"), lax.axis_index("win")
    z, x, core = chan // 4, (chan // 2) % 2, chan % 2
    first_x = x + (1 - core) * (1 - 2 * x)
    first_win = win + core * (1 - 2 * win)
    second_x = x + core * (1 - 2 * x)
    second_win = win + (1 - core) * (1 - 2 * win)

    def device(z, x, core, win):
        return (z * 4 + x * 2 + core, win)

    def block(z, x, core, win):
        return (z * 4 + x * 2 + core) * 2 + win

    first = device(z, first_x, core, first_win)
    second = device(z, second_x, core, second_win)
    sibling = device(z, x, 1 - core, win)
    up, down = device(z + 1, x, core, win), device(z - 1, x, core, win)
    has_up, has_down = z + 1 < line, z >= 1

    barrier = pltpu.get_barrier_semaphore()

    def greet(partner):
        pl.semaphore_signal(
            barrier, inc=1, device_id=partner, device_id_type=pl.DeviceIdType.MESH
        )

    for partner in (first, second, sibling):
        greet(partner)
    when(has_up, functools.partial(greet, up))
    when(has_down, functools.partial(greet, down))
    levels_beside = (z + line - 1) // line + (2 * line - 2 - z) // line
    pl.semaphore_wait(barrier, 3 + levels_beside)

    started = []

    def part(ref, half):
        rows = src_ref.shape[0] // HALVES
        return ref.at[pl.ds(half * rows, rows)]

    def send(target, number, half, present, own=False):
        copy = pltpu.make_async_remote_copy(
            src_ref=part(src_ref if own else out_ref.at[number], half),
            dst_ref=part(out_ref.at[number], half),
            send_sem=send_sem.at[len(started)],
            recv_sem=recv_sem.at[number * HALVES + half],
            device_id=target,
            device_id_type=pl.DeviceIdType.MESH,
        )
        started.append((present, copy))
        when(present, copy.start)

    def arrived(number, half):
        pltpu.make_async_remote_copy(
            src_ref=part(out_ref.at[number], half),
            dst_ref=part(out_ref.at[number], half),
            send_sem=send_sem.at[0],
            recv_sem=recv_sem.at[number * HALVES + half],
            device_id=sibling,
            device_id_type=pl.DeviceIdType.MESH,
        ).wait_recv()

    lags, rows, length = held.shape[1:]
    samples = length // windows
    chunks = x_ref.shape[0] // rows
    spot = lax.broadcasted_iota(jnp.int32, (rows, samples), 1)

    def write(slot, chunk):
        return pltpu.make_async_copy(
            held.at[slot],
            lagged_ref.at[:, pl.ds(pl.multiple_of(chunk * rows, rows), rows), :],
            out_sem.at[slot],
        )

    def shift_chunk(chunk, carry):
        slot = chunk % 2

        @pl.when(chunk >= 2)
        def _():
            write(slot, chunk - 2).wait()

        for w in range(windows):
            part = x_ref[
                pl.ds(pl.multiple_of(chunk * rows, rows), rows), w * samples : (w + 1) * samples
            ].astype(jnp.float32)
            for index, lag in enumerate(LAG_ORDER):
                held[slot, index, :, w * samples : (w + 1) * samples] = moved_rows(
                    part, spot, lag
                ).astype(jnp.bfloat16)
        write(slot, chunk).start()
        return carry

    own = block(z, x, core, win)
    mine = pltpu.make_async_copy(src_ref, out_ref.at[own], local_sem)
    for half in range(HALVES):
        send(up, own, half, has_up, own=True)
        send(down, own, half, has_down, own=True)
        for target in (first, second, sibling):
            send(target, own, half, None, own=True)
    mine.start()
    groups = [[(z, None, None, None)]]
    for r in range(1, line):
        groups.append([(z - r, z >= r, up, has_up), (z + r, z + r < line, down, has_down)])

    def from_level(group):
        for half, (level, present, onward, further) in itertools.product(range(HALVES), group):
            number = block(level, x, core, win)
            when(present, functools.partial(arrived, number, half))
            send(onward, number, half, jnp.logical_and(present, further))
            for target in (first, second, sibling):
                send(target, number, half, present)

    def from_first(group):
        for half, (level, present, _, _) in itertools.product(range(HALVES), group):
            number = block(level, first_x, core, first_win)
            when(present, functools.partial(arrived, number, half))
            for target in (second, sibling):
                send(target, number, half, present)

    def from_second(group, px, pwin):
        for half, (level, present, _, _) in itertools.product(range(HALVES), group):
            number = block(level, px, core, pwin)
            when(present, functools.partial(arrived, number, half))
            send(sibling, number, half, present)

    share = chunks // (2 * line)
    done = 0
    for k in range(1, line + 2):
        if k < line:
            from_level(groups[k])
        if k <= line:
            lax.fori_loop(done, done + share, shift_chunk, 0)
            done += share
            from_first(groups[k - 1])
            lax.fori_loop(done, done + share, shift_chunk, 0)
            done += share
            from_second(groups[k - 1], second_x, second_win)
        if k >= 2:
            from_second(groups[k - 2], 1 - x, 1 - win)
    if done < chunks:
        lax.fori_loop(done, chunks, shift_chunk, 0)
    for level in range(line):
        for px, pwin in [(x, win), (first_x, first_win), (second_x, second_win), (1 - x, 1 - win)]:
            for half in range(HALVES):
                arrived(block(level, px, 1 - core, pwin), half)
    for chunk in range(max(0, chunks - 2), chunks):
        write(chunk % 2, chunk).wait()
    mine.wait()
    for present, copy in started:
        when(present, copy.wait_send)


def gather_and_shift(sources, receivers, blocks, windows):
    line = blocks // 4
    channels, length = receivers.shape
    rows = 16
    devices = blocks * windows
    whole = pl.BlockSpec(memory_space=pl.ANY)
    gathered, lagged = pl.pallas_call(
        functools.partial(gather_kernel, line, windows),
        out_shape=(
            jax.ShapeDtypeStruct((devices, *sources.shape), jnp.bfloat16),
            jax.ShapeDtypeStruct((LAGS, channels, length), jnp.bfloat16),
        ),
        in_specs=[whole, pl.BlockSpec(memory_space=pltpu.VMEM)],
        out_specs=(whole, whole),
        scratch_shapes=[
            pltpu.VMEM((2, LAGS, rows, length), jnp.bfloat16),
            pltpu.SemaphoreType.DMA,
            pltpu.SemaphoreType.DMA((16 * line * HALVES,)),
            pltpu.SemaphoreType.DMA((devices * HALVES,)),
            pltpu.SemaphoreType.DMA((2,)),
        ],
        compiler_params=pltpu.CompilerParams(
            collective_id=0, has_side_effects=True, vmem_limit_bytes=12 * 1024 * 1024
        ),
        name="gather_and_shift",
    )(sources, receivers)
    return gathered.reshape(blocks, VIRTUAL_SOURCES, length), lagged


def correlate_kernel(factor, partner, limit, lhs_ref, *refs):
    source_refs, out_ref = refs[:-1], refs[-1]
    slots = len(source_refs)
    _, rows, length = lhs_ref.shape

    def columns(index):
        low = (LAG_ORDER[index] + MAXIMUM_LAG) * VIRTUAL_SOURCES
        return slice(low, low + VIRTUAL_SOURCES)

    def multiply(group, low, high):
        panel = jnp.concatenate([source_refs[k][0] for k in group], axis=0)
        product = lax.dot_general(
            lhs_ref[low:high].reshape((high - low) * rows, length),
            panel,
            (((1,), (1,)), ((), ())),
            preferred_element_type=jnp.float32,
        )
        for index in range(low, high):
            for i, k in enumerate(group):
                piece = product[
                    (index - low) * rows : (index - low + 1) * rows,
                    i * VIRTUAL_SOURCES : (i + 1) * VIRTUAL_SOURCES,
                ]
                kept = abs(LAG_ORDER[index]) <= limit[k]
                out_ref[k, :, columns(index)] = jnp.where(kept, piece * factor, 0.0)

    def clear(group, low, high):
        for index in range(low, high):
            for k in group:
                out_ref[k, :, columns(index)] = jnp.zeros((rows, VIRTUAL_SOURCES), jnp.float32)

    for first in range(0, slots, 2):
        group = range(first, min(first + 2, slots))
        reach = functools.reduce(jnp.maximum, [limit[k] for k in group])
        for low, high in ((0, NEAR), (NEAR, LAGS)):
            needed = reach >= abs(LAG_ORDER[low])
            pl.when(needed)(functools.partial(multiply, group, low, high))
            pl.when(jnp.logical_not(needed))(functools.partial(clear, group, low, high))


def correlate(lagged, gathered, partner, limit):
    _, channels, length = lagged.shape
    slots = partner.shape[0]
    rows = min(64, channels)
    held = 2 * length * (LAGS * rows + slots * VIRTUAL_SOURCES)
    held += 4 * slots * rows * LAGS * VIRTUAL_SOURCES
    limit_bytes = min(VMEM_LIMIT, 2 * held + 6 * 1024 * 1024)

    def source_spec(k):
        return pl.BlockSpec(
            (1, VIRTUAL_SOURCES, length), lambda c, partner, limit: (partner[k], 0, 0)
        )

    return pl.pallas_call(
        functools.partial(correlate_kernel, 1.0 / math.sqrt(length)),
        grid_spec=pltpu.PrefetchScalarGridSpec(
            num_scalar_prefetch=2,
            grid=(channels // rows,),
            in_specs=[pl.BlockSpec((LAGS, rows, length), lambda c, partner, limit: (0, c, 0))]
            + [source_spec(k) for k in range(slots)],
            out_specs=pl.BlockSpec(
                (slots, rows, LAGS * VIRTUAL_SOURCES), lambda c, partner, limit: (0, c, 0)
            ),
        ),
        out_shape=jax.ShapeDtypeStruct((slots, channels, LAGS * VIRTUAL_SOURCES), jnp.float32),
        compiler_params=pltpu.CompilerParams(vmem_limit_bytes=limit_bytes),
        name="correlate",
    )(partner, limit, lagged, *[gathered] * slots)


def gather_by_window(sources, partner, windows):
    samples = sources.shape[1] // windows
    blocks = lax.axis_size("chan")

    def one(window, panels):
        mine = lax.dynamic_slice_in_dim(sources, window * samples, samples, 1)
        mine = lax.all_gather(mine, "win", tiled=True)
        taken = lax.all_gather(mine, "chan")[partner]
        return lax.dynamic_update_slice_in_dim(panels, taken, window * samples, 2)

    empty = jnp.zeros((partner.shape[0], VIRTUAL_SOURCES, sources.shape[1]), sources.dtype)
    return lax.fori_loop(0, windows, one, empty)


def on_device(strain_rate, bandpass_taps, pair_offsets, lag_limit):
    blocks, windows = lax.axis_size("chan"), lax.axis_size("win")
    _, rows, total = strain_rate.shape
    channels = total // (blocks * windows)
    if windows > 2:
        parts = lax.all_to_all(
            strain_rate[0], ("chan", "win"), split_axis=1, concat_axis=0, tiled=True
        ).reshape(blocks, windows, rows, channels)
        receivers, sources = normalize(parts, bandpass_taps)
    else:
        receivers, sources = exchange_and_normalize(
            strain_rate[0], bandpass_taps, blocks, windows
        )
    offsets = pair_offsets[0]
    used = offsets >= 0
    partner = jnp.where(used, (lax.axis_index("chan") + offsets) % blocks, 0).astype(jnp.int32)
    limit = jnp.where(used, lag_limit[0], -1).astype(jnp.int32)
    if windows > 2:
        lagged = shift(receivers, windows)
        panels = gather_by_window(sources, partner, windows)
        return correlate(lagged, panels, jnp.arange(partner.shape[0], dtype=jnp.int32), limit)
    gathered, lagged = gather_and_shift(sources, receivers, blocks, windows)
    return correlate(lagged, gathered, partner, limit)


def solution(mesh):
    placed = (P("win", "chan", None), P(), P("chan", None), P("chan", None))
    return jax.shard_map(
        on_device,
        mesh=mesh,
        in_specs=placed,
        out_specs=P(None, ("chan", "win"), None),
        check_vma=False,
    )
```
